128 devices in a mesh: phase: 2 (over x_hi), seq: 64 (over z, y, x_lo, core).
Axes of the slice: x: 4 (x_hi: 2, x_lo: 2; x = x_hi * 2 + x_lo), y: 4, z: 4, core: 2. Of those that a mesh axis runs over, the one named last changes fastest.
Arguments:
- dec_in: bfloat16 [2, 512, 4096], P(None, None, 'seq'), may hold values from -6 to 6
- enc_kv: bfloat16 [2, 2, 8192, 8192], P('phase', None, 'seq'), may hold values from -15 to 15
- dec_seg: int32 [2, 512], replicated, may hold values from 0 to 3, never falling along the last dimension, each value on 1 to 256 neighbouring positions
- enc_seg: int32 [2, 8192], replicated, may hold values from 0 to 3, never falling along the last dimension, each value on 1 to 4096 neighbouring positions
- q_gain: float32 [2, 4096], P('phase', 'seq'), may hold values from 0.5 to 1.5
- o_gain: float32 [2, 4096], P('phase', 'seq'), may hold values from 1 to 8
- cotangent: bfloat16 [2, 512, 4096], P(None, None, 'seq'), may hold values from -6 to 6
Outputs:
- sect_out: bfloat16 [2, 2, 512, 4096], P('phase', None, None, 'seq')
- grad_kv: bfloat16 [2, 2, 8192, 8192], P('phase', None, 'seq')
- grad_q_gain: float32 [2, 4096], P('phase', 'seq')
- grad_o_gain: float32 [2, 4096], P('phase', 'seq')
The draws below stay inside these ranges and needn't reach their ends.
Inputs may be any that keep to these rules, and one draw needn't show every extreme that they name: `dec_seg`: every one of the 4 documents has positions in both the decoder and the encoder of each micro-batch.
All inputs are finite; a program needn't handle non-finite values.
Results may differ from the reference program's by a relative error of at most 0.0075.
The reference program's roundings to bfloat16 on the way count: a program that leaves them out, or rounds other values in their place, can miss the bound.
Values may be sent and summed in bfloat16 or wider, within the bound.
No kernel may reach another device: no remote copies, remote signals or barrier semaphores. Data moves between devices by JAX's collectives and lax.ppermute only.
A program may use at most 192 MiB of HBM per device.

```python
import math
import jax
import jax.numpy as jnp
import numpy as np
from jax import lax

D = 4096
HEADS = 64
HEAD = 64
DEC_TOK = 512
MICRO = 2
DOCS = 4
ENC_TOK = 8192
SECTIONS = 2


def steps_of(key, extent, cuts, smallest, top_value):
    loudness = 1.0
    for position, parts in cuts:
        steps = jax.random.uniform(jax.random.fold_in(jax.random.fold_in(key, 6), position), (parts,), jnp.float32, smallest / len(cuts), top_value / len(cuts))
        loudness = loudness * jnp.repeat(jnp.exp(steps), extent[position] // parts).reshape((-1,) + (1,) * (len(extent) - 1 - position))
    return loudness


def profile(count, total, bound, slope):
    portions = [(1 << 20) // math.isqrt(rank ** slope) + 1 for rank in range(2, count + 1)]
    rest, counts = total - bound - (count - 1), [1] * (count - 1)
    while rest > 0:
        candidates = [i for i in range(count - 1) if counts[i] < bound]
        whole, left = sum([portions[i] for i in candidates]), rest
        for i in candidates:
            extra = min(bound - counts[i], max(1, left * portions[i] // whole), rest)
            counts[i] = counts[i] + extra
            rest = rest - extra
    return np.array([bound] + counts)


def uneven(key, amount, total, bound, skew):
    if amount == 2:
        one = jax.random.randint(key, (), max(1, total - bound), min(bound, total - 1) + 1)
        return jnp.stack([one, total - one])
    tallies = jnp.asarray(profile(amount, total, bound, skew), jnp.int32)
    pairs = (amount - 1) // 2
    source_of, taker = tallies[1:1 + 2 * pairs:2], tallies[2:2 + 2 * pairs:2]
    room = jnp.minimum(source_of - 1, bound - taker)
    passed = jax.random.randint(jax.random.fold_in(key, 1), (pairs,), 0, 1 << 20) % (room + 1)
    tallies = tallies.at[1:1 + 2 * pairs:2].set(source_of - passed).at[2:2 + 2 * pairs:2].set(taker + passed)
    return tallies[jax.random.permutation(jax.random.fold_in(key, 2), amount)]


def scatter_about(key, dims, spread, limit, cuts=(), kind=jnp.bfloat16):
    result = jax.random.normal(key, dims, jnp.float32) * spread
    if len(cuts) > 0:
        result = steps_of(key, dims, cuts, -0.22, 0.18) * result
    return jnp.clip(result, min=-limit, max=limit).astype(kind)


def setup_inputs(seed: int = 0) -> dict:
    seeds = jax.random.split(jax.random.key(seed), 8)
    dec_in = scatter_about(seeds[0], (MICRO, DEC_TOK, D), 1.0, 6.0, ((2, 64),))
    enc_kv = scatter_about(seeds[1], (SECTIONS, MICRO, ENC_TOK, 2 * D), 2.5, 15.0, ((0, 2), (2, 64)))
    dec_seg = jax.vmap(lambda own: jnp.searchsorted(jnp.cumsum(uneven(own, DOCS, DEC_TOK, DEC_TOK // 2, 2)), jnp.arange(DEC_TOK), side="right"))(jax.random.split(seeds[2], MICRO)).reshape((MICRO, DEC_TOK)).astype(jnp.int32)
    enc_seg = jax.vmap(lambda own: jnp.searchsorted(jnp.cumsum(uneven(own, DOCS, ENC_TOK, ENC_TOK // 2, 2)), jnp.arange(ENC_TOK), side="right"))(jax.random.split(seeds[3], MICRO)).reshape((MICRO, ENC_TOK)).astype(jnp.int32)
    q_gain = jnp.clip(1.0 + 0.1 * jax.random.normal(seeds[4], (SECTIONS, D), jnp.float32), 0.5, 1.5)
    o_gain = jnp.clip(jnp.exp(math.log(8.0) - 2.0794415 * jax.random.uniform(seeds[5], (SECTIONS, D), jnp.float32) ** steps_of(seeds[5], (SECTIONS, D), ((0, 2), (1, 64)), -0.2, 0.2)), 1.0, 8.0)
    cotangent = scatter_about(seeds[6], (MICRO, DEC_TOK, D), 1.0, 6.0, ((2, 64),))
    return dict(dec_in=dec_in, enc_kv=enc_kv, dec_seg=dec_seg, enc_seg=enc_seg, q_gain=q_gain, o_gain=o_gain, cotangent=cotangent)


eps = 1e-06
neg_big = -1e+30

def head_forward(query, keys, values, allowed):
    scale = 1.0 / math.sqrt(HEAD)
    scores = jnp.dot(query, keys.T, preferred_element_type=jnp.float32) * scale
    scores = jnp.where(allowed, scores, neg_big)
    top = lax.optimization_barrier(jnp.max(scores, axis=1, keepdims=True))
    expo = jnp.exp(scores - top)
    probs = expo / lax.optimization_barrier(jnp.sum(expo, axis=1, keepdims=True))
    weights = probs.astype(jnp.bfloat16)
    output = jnp.dot(weights, values, preferred_element_type=jnp.float32)
    return (output, probs, weights)

def head_backward(query, keys, values, allowed, grad_out):
    scale = 1.0 / math.sqrt(HEAD)
    output, probs, weights = head_forward(query, keys, values, allowed)
    grad_low = grad_out.astype(jnp.bfloat16)
    grad_values = jnp.dot(weights.T, grad_low, preferred_element_type=jnp.float32)
    grad_probs = jnp.dot(grad_low, values.T, preferred_element_type=jnp.float32)
    delta = lax.optimization_barrier(jnp.sum(probs * grad_probs, axis=1, keepdims=True))
    grad_scores = (probs * (grad_probs - delta) * scale).astype(jnp.bfloat16)
    grad_query = jnp.dot(grad_scores, keys, preferred_element_type=jnp.float32)
    grad_keys = jnp.dot(grad_scores.T, query, preferred_element_type=jnp.float32)
    return (output, grad_query, grad_keys, grad_values)

def prepare(x, qgain):
    xf = x.astype(jnp.float32)
    total = lax.optimization_barrier(jnp.sum(xf * xf, axis=1))
    inv = lax.rsqrt(total / D + eps)
    normed = xf * inv[:, None]
    query = (normed * qgain[None, :]).astype(jnp.bfloat16)
    return (xf, inv, normed, query)

def by_heads(array):
    return jnp.transpose(array.reshape(array.shape[0], HEADS, HEAD), (1, 0, 2))

def section_forward(x, keyval, allowed, qgain, ogain):
    xf, inv, normed, query = prepare(x, qgain)
    keys = jnp.transpose(keyval[:, :, 0, :], (1, 0, 2))
    values = jnp.transpose(keyval[:, :, 1, :], (1, 0, 2))

    def one_head(item):
        return head_forward(item[0], item[1], item[2], allowed)[0]
    output = lax.map(one_head, (by_heads(query), keys, values))
    output = jnp.transpose(output, (1, 0, 2)).reshape(x.shape[0], D)
    return (xf + ogain[None, :] * output).astype(jnp.bfloat16)

def section_backward(x, keyval, allowed, qgain, ogain, grad_y):
    xf, inv, normed, query = prepare(x, qgain)
    keys = jnp.transpose(keyval[:, :, 0, :], (1, 0, 2))
    values = jnp.transpose(keyval[:, :, 1, :], (1, 0, 2))
    grad_f = grad_y.astype(jnp.float32)
    grad_out = grad_f * ogain[None, :]

    def one_head(item):
        return head_backward(item[0], item[1], item[2], allowed, item[3])
    output, grad_query, grad_keys, grad_values = lax.map(one_head, (by_heads(query), keys, values, by_heads(grad_out)))
    rows = x.shape[0]
    output = jnp.transpose(output, (1, 0, 2)).reshape(rows, D)
    grad_query = jnp.transpose(grad_query, (1, 0, 2)).reshape(rows, D)
    grad_pair = jnp.transpose(jnp.stack([grad_keys, grad_values], axis=2), (1, 0, 2, 3))
    grad_pair = grad_pair.reshape(grad_pair.shape[0], 2 * D).astype(jnp.bfloat16)
    grad_qg = lax.optimization_barrier(jnp.sum(grad_query * normed, axis=0))
    grad_og = lax.optimization_barrier(jnp.sum(grad_f * output, axis=0))
    grad_normed = grad_query * qgain[None, :]
    cross = lax.optimization_barrier(jnp.sum(grad_normed * xf, axis=1))
    grad_x = grad_f + inv[:, None] * grad_normed - xf * (inv * inv * inv)[:, None] * (cross / D)[:, None]
    return (grad_x.astype(jnp.bfloat16), grad_pair, grad_qg, grad_og)

def reference(dec_in, enc_kv, dec_seg, enc_seg, q_gain, o_gain, cotangent):
    outs = [[None] * MICRO for s in range(SECTIONS)]
    inputs = [[None] * MICRO for s in range(SECTIONS)]
    for m in range(MICRO):
        allowed = dec_seg[m][:, None] == enc_seg[m][None, :]
        x = dec_in[m]
        for s in range(SECTIONS):
            keyval = enc_kv[s, m].reshape(ENC_TOK, HEADS, 2, HEAD)
            inputs[s][m] = x
            x = section_forward(x, keyval, allowed, q_gain[s], o_gain[s])
            outs[s][m] = x
    grads = [[None] * MICRO for s in range(SECTIONS)]
    qg_sum = [jnp.zeros((D,), jnp.float32) for s in range(SECTIONS)]
    og_sum = [jnp.zeros((D,), jnp.float32) for s in range(SECTIONS)]
    for m in range(MICRO):
        allowed = dec_seg[m][:, None] == enc_seg[m][None, :]
        grad_y = cotangent[m]
        for s in reversed(range(SECTIONS)):
            keyval = enc_kv[s, m].reshape(ENC_TOK, HEADS, 2, HEAD)
            grad_y, grad_pair, grad_qg, grad_og = section_backward(inputs[s][m], keyval, allowed, q_gain[s], o_gain[s], grad_y)
            grads[s][m] = grad_pair
            qg_sum[s] = qg_sum[s] + grad_qg
            og_sum[s] = og_sum[s] + grad_og
    sect_out = jnp.stack([jnp.stack(outs[s]) for s in range(SECTIONS)])
    grad_kv = jnp.stack([jnp.stack(grads[s]) for s in range(SECTIONS)])
    return (sect_out, grad_kv, jnp.stack(qg_sum), jnp.stack(og_sum))
```

```python
import functools
import math

import jax
import jax.numpy as jnp
from jax import lax
from jax.experimental import pallas as pl
from jax.experimental.pallas import tpu as pltpu
from jax.sharding import PartitionSpec as P

D = 4096
HEAD = 64
EPS = 1e-06
NEG = -1e30
TILE = 128
CHUNK = 512
TAIL = 16
SCALE = 1.0 / math.sqrt(HEAD)
LOG2 = SCALE * math.log2(math.e)
BOTH = ("phase", "seq")
F32 = jnp.float32
BF16 = jnp.bfloat16


def dot(a, b, ca, cb):
    return lax.dot_general(a, b, (((ca,), (cb,)), ((), ())), preferred_element_type=F32)


def vmem(shape, index):
    return pl.BlockSpec(shape, lambda i: index)


def whole(shape):
    return vmem(shape, (0,) * len(shape))


SMEM = pl.BlockSpec(memory_space=pltpu.SMEM)
PARAMS = dict(
    compiler_params=pltpu.CompilerParams(
        dimension_semantics=("arbitrary",), vmem_limit_bytes=48 * 1024 * 1024
    )
)


def pack_kernel(phase_ref, kv_ref, x_ref, out_ref):
    heads = kv_ref.shape[2] // (2 * HEAD)
    for h in range(heads):
        out_ref[h, 0:128, :] = kv_ref[0, :, h * 128 : (h + 1) * 128]
    x = x_ref[0, pl.ds(phase_ref[0] * 256, 256), :].astype(F32)
    x = jnp.concatenate([x, jnp.zeros_like(x)], axis=1)
    xt = jnp.transpose(x)
    total = jnp.sum(xt * xt, axis=0, keepdims=True)
    rows = []
    for _ in range(3):
        part = total.astype(BF16)
        partf = part.astype(F32)
        rows += [partf[:, 0:128], partf[:, 128:256]]
        total = total - partf
    rows.append(jnp.zeros((TAIL - 6, 128), F32))
    tail = jnp.concatenate(rows, axis=0).astype(BF16)
    for h in range(heads):
        out_ref[h, 128 : 128 + TAIL, :] = tail


def pack(phase, kv, dec_in):
    micro, rows, feats = kv.shape
    parts = 4
    heads = feats // 128 // parts
    return pl.pallas_call(
        pack_kernel,
        grid=(micro * parts,),
        in_specs=[
            SMEM,
            pl.BlockSpec((1, rows, feats // parts), lambda i: (i // parts, 0, i % parts)),
            pl.BlockSpec((1, dec_in.shape[1], HEAD), lambda i: (i // parts, 0, 0)),
        ],
        out_specs=pl.BlockSpec((heads, rows + TAIL, 128), lambda i: (i, 0, 0)),
        out_shape=jax.ShapeDtypeStruct((micro * parts * heads, rows + TAIL, 128), BF16),
        name="pack",
        **PARAMS,
    )(phase, kv, dec_in)


def unpack_kernel(in_ref, out_ref):
    for h in range(in_ref.shape[0]):
        out_ref[0, :, h * 128 : (h + 1) * 128] = in_ref[h]


def unpack(blocks, micro):
    count, rows, _ = blocks.shape
    parts = 4
    heads = count // micro // parts
    return pl.pallas_call(
        unpack_kernel,
        grid=(micro * parts,),
        in_specs=[pl.BlockSpec((heads, rows, 128), lambda i: (i, 0, 0))],
        out_specs=pl.BlockSpec((1, rows, heads * 128), lambda i: (i // parts, 0, i % parts)),
        out_shape=jax.ShapeDtypeStruct((micro, rows, parts * heads * 128), BF16),
        name="unpack",
        **PARAMS,
    )(blocks)


def chunk_of(kv_ref, c):
    per = CHUNK // 128
    return kv_ref[0, pl.ds(c * per, per)].reshape(CHUNK, 128)


def at(c):
    return pl.ds(pl.multiple_of(c * CHUNK, CHUNK), CHUNK)


def lanes(t):
    return slice(t * TILE, (t + 1) * TILE)


def logits(product, c, first, last):
    position = lax.broadcasted_iota(jnp.int32, product.shape, 0) + c * CHUNK
    allowed = (position >= first) & (position < last)
    return jnp.where(allowed, product * LOG2, NEG)


def forward_tile(bounds_ref, kv_ref, t, query, first, last, store, keep_probs):
    lo, hi = bounds_ref[t], bounds_ref[4 + t]

    def stats(c, carry):
        top, norm = carry
        scores = logits(dot(chunk_of(kv_ref, c), query, 1, 0), c, first, last)
        store[at(c), :] = scores
        groups = scores.reshape(CHUNK // 8, 8, TILE)
        now = jnp.maximum(top, jnp.max(groups, axis=0))
        norm = norm * jnp.exp2(top - now) + jnp.sum(jnp.exp2(groups - now[None]), axis=0)
        return now, norm

    top, norm = lax.fori_loop(
        lo, hi, stats, (jnp.full((8, TILE), NEG, F32), jnp.zeros((8, TILE), F32))
    )
    peak = jnp.max(top, axis=0, keepdims=True)
    lse = peak + jnp.log2(jnp.sum(norm * jnp.exp2(top - peak), axis=0, keepdims=True))

    def gather(c, total):
        probs = jnp.exp2(store[at(c), :] - lse)
        if keep_probs:
            store[at(c), :] = probs
        weights = probs.astype(BF16)
        rest = (probs - weights.astype(F32)).astype(BF16)
        return total + dot(
            chunk_of(kv_ref, c), jnp.concatenate([weights, rest], axis=1), 0, 0
        )

    total = lax.fori_loop(lo, hi, gather, jnp.zeros((128, 2 * TILE), F32))
    attn = total[HEAD:, :TILE]
    return lse, attn, attn + total[HEAD:, TILE:]


def pad_low(a):
    return jnp.concatenate([a, jnp.zeros_like(a)], axis=0)


def pad_high(a):
    return jnp.concatenate([jnp.zeros_like(a), a], axis=0)


def upright(a):
    return jnp.transpose(a.astype(F32)).astype(BF16)


def normed_query(xt, total, qgain):
    inv = lax.rsqrt(total / D + EPS)
    return inv, (xt * inv * qgain).astype(BF16)


def forward_kernel(
    bounds_ref, kv_ref, tails_ref, xt_ref, range_ref, qgain_ref, ogain_ref,
    out_ref, sums_ref, lse_ref, attn_ref, exact_ref, inv_ref, store,
):
    tails = jnp.sum(tails_ref[...].astype(F32), axis=1)
    pieces = []
    for half in range(2):
        pieces += [
            tails[half, j : j + 1] + tails[half, j + 2 : j + 3] + tails[half, j + 4 : j + 5]
            for j in range(2)
        ]
    total = jnp.concatenate(pieces, axis=1)
    xt = xt_ref[...].astype(F32)
    inv, query = normed_query(xt, total, qgain_ref[...])
    inv_ref[...] = inv
    query = pad_low(query)
    for t in range(4):
        s = lanes(t)
        lse, attn, exact = forward_tile(
            bounds_ref, kv_ref, t, query[:, s], range_ref[0:1, s], range_ref[1:2, s], store, False
        )
        lse_ref[:, s] = lse
        attn_ref[:, s] = attn
        exact_ref[:, s] = exact
        out_ref[:, s] = (xt[:, s] + ogain_ref[...] * attn).astype(BF16)
    out = out_ref[...].astype(F32)
    sums_ref[...] = jnp.broadcast_to(jnp.sum(out * out, axis=0, keepdims=True), sums_ref.shape)


def forward(bounds, received, xt, ranges, qgain, ogain):
    rows = xt.shape[1]
    blocks = received.shape[1]
    return pl.pallas_call(
        forward_kernel,
        grid=(1,),
        in_specs=[
            SMEM,
            vmem((1, blocks, 128, 128), (0, 0, 0, 0)),
            vmem((2, blocks, TAIL, 128), (0, 0, 128 // TAIL, 0)),
            whole((HEAD, rows)),
            whole((2, rows)),
            whole((HEAD, 1)),
            whole((HEAD, 1)),
        ],
        out_specs=[
            whole((HEAD, rows)),
            whole((blocks, rows)),
            whole((1, rows)),
            whole((HEAD, rows)),
            whole((HEAD, rows)),
            whole((1, rows)),
        ],
        out_shape=[
            jax.ShapeDtypeStruct((HEAD, rows), BF16),
            jax.ShapeDtypeStruct((blocks, rows), F32),
            jax.ShapeDtypeStruct((1, rows), F32),
            jax.ShapeDtypeStruct((HEAD, rows), F32),
            jax.ShapeDtypeStruct((HEAD, rows), F32),
            jax.ShapeDtypeStruct((1, rows), F32),
        ],
        scratch_shapes=[pltpu.VMEM((blocks * 128, TILE), F32)],
        name="forward",
        **PARAMS,
    )(bounds, received, received, xt, ranges, qgain, ogain)


def backward_step(keyval, probs, grad_probs, delta, pair, summed, c):
    grad_scores = (probs * (grad_probs - delta)).astype(BF16)
    left = jnp.concatenate([grad_scores, probs.astype(BF16)], axis=1)
    summed[at(c), :] += dot(left, pair, 1, 0)
    return dot(keyval, grad_scores, 0, 0)


def middle_kernel(
    bounds_ref, kv_ref, sums_ref, xt_ref, range_ref, qgain_ref, ogain_ref, gt_ref,
    grad_kv_ref, out_ref, cross_ref, grad_norm_ref, inv_ref, grad_qg_ref, grad_og_ref,
    store, summed, attn_ref, grad_query_ref,
):
    summed[...] = jnp.zeros_like(summed)
    total = jnp.sum(sums_ref[...], axis=0, keepdims=True)
    xt = xt_ref[...].astype(F32)
    inv, low = normed_query(xt, total, qgain_ref[...])
    inv_ref[...] = inv
    query = pad_low(low)
    keys_side = upright(query.astype(F32) * SCALE)
    grad = gt_ref[...].astype(F32)
    grad_low = (grad * ogain_ref[...]).astype(BF16)
    grad_out = pad_high(grad_low)
    values_side = upright(grad_out)
    for t in range(4):
        s = lanes(t)
        lse, attn, exact = forward_tile(
            bounds_ref, kv_ref, t, query[:, s], range_ref[0:1, s], range_ref[1:2, s], store, True
        )
        attn_ref[:, s] = attn
        delta = jnp.sum(grad_low[:, s].astype(F32) * exact, axis=0, keepdims=True)
        pair = jnp.concatenate([keys_side[s], values_side[s]], axis=0)
        grad_tile = grad_out[:, s]

        def back(c, grad_query):
            keyval = chunk_of(kv_ref, c)
            grad_probs = dot(keyval, grad_tile, 1, 0)
            return grad_query + backward_step(
                keyval, store[at(c), :], grad_probs, delta, pair, summed, c
            )

        grad_query = lax.fori_loop(
            bounds_ref[t], bounds_ref[4 + t], back, jnp.zeros((128, TILE), F32)
        )
        grad_query_ref[:, s] = grad_query[:HEAD] * SCALE
    attn = attn_ref[...]
    out_ref[...] = (xt + ogain_ref[...] * attn).astype(BF16)
    grad_query = grad_query_ref[...]
    grad_norm = grad_query * qgain_ref[...]
    grad_norm_ref[...] = grad_norm
    cross = jnp.sum(grad_norm * xt, axis=0, keepdims=True)
    cross_ref[...] = jnp.broadcast_to(cross, cross_ref.shape)
    grad_qg_ref[...] = jnp.sum(grad_query * (xt * inv), axis=1, keepdims=True)
    grad_og_ref[...] = jnp.sum(grad * attn, axis=1, keepdims=True)
    grad_kv_ref[...] = summed[...].reshape(grad_kv_ref.shape).astype(BF16)


def middle(bounds, received, sums, xt, ranges, qgain, ogain, gt):
    rows = xt.shape[1]
    blocks = received.shape[1]
    return pl.pallas_call(
        middle_kernel,
        grid=(1,),
        in_specs=[
            SMEM,
            vmem((1, blocks, 128, 128), (1, 0, 0, 0)),
            whole((blocks, rows)),
            whole((HEAD, rows)),
            whole((2, rows)),
            whole((HEAD, 1)),
            whole((HEAD, 1)),
            whole((HEAD, rows)),
        ],
        out_specs=[
            vmem((1, blocks, 128, 128), (1, 0, 0, 0)),
            whole((HEAD, rows)),
            whole((blocks, rows)),
            whole((HEAD, rows)),
            whole((1, rows)),
            whole((HEAD, 1)),
            whole((HEAD, 1)),
        ],
        out_shape=[
            jax.ShapeDtypeStruct((2, blocks, 128, 128), BF16),
            jax.ShapeDtypeStruct((HEAD, rows), BF16),
            jax.ShapeDtypeStruct((blocks, rows), F32),
            jax.ShapeDtypeStruct((HEAD, rows), F32),
            jax.ShapeDtypeStruct((1, rows), F32),
            jax.ShapeDtypeStruct((HEAD, 1), F32),
            jax.ShapeDtypeStruct((HEAD, 1), F32),
        ],
        scratch_shapes=[
            pltpu.VMEM((blocks * 128, TILE), F32),
            pltpu.VMEM((blocks * 128, 128), F32),
            pltpu.VMEM((HEAD, rows), F32),
            pltpu.VMEM((HEAD, rows), F32),
        ],
        name="middle",
        **PARAMS,
    )(bounds, received, sums, xt, ranges, qgain, ogain, gt)


def backward_kernel(
    bounds_ref, kv_ref, cross_ref, gt_ref, grad_norm_ref, xt1_ref, inv1_ref,
    xt_ref, inv_ref, lse_ref, attn_ref, exact_ref, range_ref, qgain_ref, ogain_ref, held_ref,
    grad_kv_ref, grad_qg_ref, grad_og_ref, summed, grad_query_ref,
):
    del held_ref
    summed[...] = jnp.zeros_like(summed)
    cross = jnp.sum(cross_ref[...], axis=0, keepdims=True)
    inv1 = inv1_ref[...]
    xt1 = xt1_ref[...].astype(F32)
    grad = gt_ref[...].astype(F32) + inv1 * grad_norm_ref[...]
    grad = (grad - xt1 * (inv1 * inv1 * inv1) * (cross / D)).astype(BF16).astype(F32)
    grad_low = (grad * ogain_ref[...]).astype(BF16)
    grad_out = pad_high(grad_low)
    values_side = upright(grad_out)
    attn = attn_ref[...]
    grad_og_ref[...] = jnp.sum(grad * attn, axis=1, keepdims=True)
    deltas = jnp.sum(grad_low.astype(F32) * exact_ref[...], axis=0, keepdims=True)
    xt = xt_ref[...].astype(F32)
    inv = inv_ref[...]
    normed = xt * inv
    query = pad_low((normed * qgain_ref[...]).astype(BF16))
    keys_side = upright(query.astype(F32) * SCALE)
    for t in range(4):
        s = lanes(t)
        first, last = range_ref[0:1, s], range_ref[1:2, s]
        lse, delta = lse_ref[:, s], deltas[:, s]
        both = jnp.concatenate([query[:, s], grad_out[:, s]], axis=1)
        pair = jnp.concatenate([keys_side[s], values_side[s]], axis=0)

        def back(c, grad_query):
            keyval = chunk_of(kv_ref, c)
            product = dot(keyval, both, 1, 0)
            probs = jnp.exp2(logits(product[:, :TILE], c, first, last) - lse)
            return grad_query + backward_step(
                keyval, probs, product[:, TILE:], delta, pair, summed, c
            )

        grad_query = lax.fori_loop(
            bounds_ref[t], bounds_ref[4 + t], back, jnp.zeros((128, TILE), F32)
        )
        grad_query_ref[:, s] = grad_query[:HEAD] * SCALE
    grad_qg_ref[...] = jnp.sum(grad_query_ref[...] * normed, axis=1, keepdims=True)
    grad_kv_ref[...] = summed[...].reshape(grad_kv_ref.shape).astype(BF16)


def backward(
    bounds, received, cross, gt, grad_norm, xt1, inv1, xt, inv, lse, attn, exact,
    ranges, qgain, ogain, held,
):
    rows = xt.shape[1]
    blocks = received.shape[1]
    return pl.pallas_call(
        backward_kernel,
        grid=(1,),
        in_specs=[
            SMEM,
            vmem((1, blocks, 128, 128), (0, 0, 0, 0)),
            whole((blocks, rows)),
            whole((HEAD, rows)),
            whole((HEAD, rows)),
            whole((HEAD, rows)),
            whole((1, rows)),
            whole((HEAD, rows)),
            whole((1, rows)),
            whole((1, rows)),
            whole((HEAD, rows)),
            whole((HEAD, rows)),
            whole((2, rows)),
            whole((HEAD, 1)),
            whole((HEAD, 1)),
            pl.BlockSpec(memory_space=pl.ANY),
        ],
        out_specs=[
            vmem((1, blocks, 128, 128), (0, 0, 0, 0)),
            whole((HEAD, 1)),
            whole((HEAD, 1)),
        ],
        out_shape=[
            jax.ShapeDtypeStruct(held.shape, BF16),
            jax.ShapeDtypeStruct((HEAD, 1), F32),
            jax.ShapeDtypeStruct((HEAD, 1), F32),
        ],
        scratch_shapes=[
            pltpu.VMEM((blocks * 128, 128), F32),
            pltpu.VMEM((HEAD, rows), F32),
        ],
        input_output_aliases={15: 0},
        name="backward",
        **PARAMS,
    )(bounds, received, cross, gt, grad_norm, xt1, inv1, xt, inv, lse, attn, exact, ranges, qgain, ogain, held)


def swap(value):
    return lax.ppermute(value, "phase", [(0, 1), (1, 0)])


def spread(value):
    return lax.all_to_all(value, "seq", 0, 0, tiled=True)


def local(dec_in, enc_kv, dec_seg, enc_seg, q_gain, o_gain, cotangent):
    phase = lax.axis_index("phase")
    first_phase = phase == 0
    micro = dec_in.shape[0]
    rows = dec_in.shape[1]
    positions = enc_seg.shape[1]
    blocks = positions // 128

    sent = pack(phase.reshape(1), enc_kv[0], dec_in)
    own = jnp.concatenate([q_gain, o_gain], axis=0)
    other = swap(own)
    received = lax.all_to_all(sent, BOTH, 0, 0, tiled=True)
    received = received.reshape(2, blocks, 128 + TAIL, 128)

    gains0 = jnp.where(first_phase, own, other)
    gains1 = jnp.where(first_phase, other, own)
    qgain0, ogain0 = gains0[0][:, None], gains0[1][:, None]
    qgain1, ogain1 = gains1[0][:, None], gains1[1][:, None]
    xt0 = lax.dynamic_index_in_dim(dec_in, phase, 0, keepdims=False).T
    gt = lax.dynamic_index_in_dim(cotangent, phase, 0, keepdims=False).T
    qseg = lax.dynamic_index_in_dim(dec_seg, phase, 0, keepdims=False)
    kseg = lax.dynamic_index_in_dim(enc_seg, phase, 0, keepdims=False)
    first = jnp.zeros((rows,), jnp.int32)
    last = jnp.zeros((rows,), jnp.int32)
    for doc in range(4):
        first = jnp.where(qseg == doc, jnp.sum((kseg < doc).astype(jnp.int32)), first)
        last = jnp.where(qseg == doc, jnp.sum((kseg <= doc).astype(jnp.int32)), last)
    ranges = jnp.stack([first, last])
    bounds = jnp.concatenate(
        [first[0::TILE] // CHUNK, (last[TILE - 1 :: TILE] + (CHUNK - 1)) // CHUNK]
    )

    xt1, sums, lse0, attn0, exact0, inv0 = forward(bounds, received, xt0, ranges, qgain0, ogain0)
    sums = spread(sums)
    grad_kv, xt2, cross, grad_norm, inv1, grad_qg1, grad_og1 = middle(
        bounds, received, sums, xt1, ranges, qgain1, ogain1, gt
    )
    cross = spread(cross)
    grad_kv, grad_qg0, grad_og0 = backward(
        bounds, received, cross, gt, grad_norm, xt1, inv1, xt0, inv0, lse0, attn0, exact0,
        ranges, qgain0, ogain0, grad_kv,
    )
    rows_back = lax.all_to_all(
        grad_kv.reshape(2 * blocks, 128, 128), BOTH, 0, 0, tiled=True
    )
    grad_rows = unpack(rows_back, micro)

    out0, out1 = xt1.T, xt2.T
    mine = jnp.where(first_phase, out0, out1)
    theirs = swap(jnp.where(first_phase, out1, out0))
    sect_out = jnp.where(
        first_phase, jnp.stack([mine, theirs]), jnp.stack([theirs, mine])
    )
    grads0 = jnp.concatenate([grad_qg0, grad_og0], axis=1).T
    grads1 = jnp.concatenate([grad_qg1, grad_og1], axis=1).T
    grads = jnp.where(first_phase, grads0, grads1) + swap(
        jnp.where(first_phase, grads1, grads0)
    )
    return (sect_out[None], grad_rows[None], grads[0:1], grads[1:2])


def solution(mesh):
    in_specs = (
        P(None, None, "seq"),
        P("phase", None, "seq", None),
        P(),
        P(),
        P("phase", "seq"),
        P("phase", "seq"),
        P(None, None, "seq"),
    )
    out_specs = (
        P("phase", None, None, "seq"),
        P("phase", None, "seq", None),
        P("phase", "seq"),
        P("phase", "seq"),
    )
    return jax.shard_map(local, mesh=mesh, in_specs=in_specs, out_specs=out_specs, check_vma=False)
```

```python
import functools
import math

import jax
import jax.numpy as jnp
from jax import lax
from jax.experimental import pallas as pl
from jax.experimental.pallas import tpu as pltpu
from jax.sharding import PartitionSpec as P

D = 4096
HEAD = 64
EPS = 1e-06
NEG = -1e30
DOCS = 4
TILE = 256
CHUNK = 512
UNROLL = 4
TAIL = 16
SCALE = 1.0 / math.sqrt(HEAD)
LOG2 = SCALE * math.log2(math.e)
BOTH = ("phase", "seq")
F32 = jnp.float32
BF16 = jnp.bfloat16


def dot(a, b, ca, cb):
    return lax.dot_general(a, b, (((ca,), (cb,)), ((), ())), preferred_element_type=F32)


def vmem(shape, index):
    return pl.BlockSpec(shape, lambda i: index)


def whole(shape):
    return vmem(shape, (0,) * len(shape))


SMEM = pl.BlockSpec(memory_space=pltpu.SMEM)
PARAMS = dict(
    compiler_params=pltpu.CompilerParams(
        dimension_semantics=("arbitrary",), vmem_limit_bytes=48 * 1024 * 1024
    )
)


def pack_kernel(phase_ref, kv_ref, x_ref, out_ref):
    heads = kv_ref.shape[2] // (2 * HEAD)
    for h in range(heads):
        out_ref[h, 0:128, :] = kv_ref[0, :, h * 128 : (h + 1) * 128]
    x = x_ref[0, pl.ds(phase_ref[0] * 256, 256), :].astype(F32)
    x = jnp.concatenate([x, jnp.zeros_like(x)], axis=1)
    xt = jnp.transpose(x)
    total = jnp.sum(xt * xt, axis=0, keepdims=True)
    rows = []
    for _ in range(3):
        part = total.astype(BF16)
        partf = part.astype(F32)
        rows += [partf[:, 0:128], partf[:, 128:256]]
        total = total - partf
    rows.append(jnp.zeros((TAIL - 6, 128), F32))
    tail = jnp.concatenate(rows, axis=0).astype(BF16)
    for h in range(heads):
        out_ref[h, 128 : 128 + TAIL, :] = tail


def pack(phase, kv, dec_in):
    micro, rows, feats = kv.shape
    parts = 4
    heads = feats // 128 // parts
    return pl.pallas_call(
        pack_kernel,
        grid=(micro * parts,),
        in_specs=[
            SMEM,
            pl.BlockSpec((1, rows, feats // parts), lambda i: (i // parts, 0, i % parts)),
            pl.BlockSpec((1, dec_in.shape[1], HEAD), lambda i: (i // parts, 0, 0)),
        ],
        out_specs=pl.BlockSpec((heads, rows + TAIL, 128), lambda i: (i, 0, 0)),
        out_shape=jax.ShapeDtypeStruct((micro * parts * heads, rows + TAIL, 128), BF16),
        name="pack",
        **PARAMS,
    )(phase, kv, dec_in)


def unpack_kernel(in_ref, out_ref):
    for h in range(in_ref.shape[0]):
        out_ref[0, :, h * 128 : (h + 1) * 128] = in_ref[h]


def unpack(blocks, micro):
    count, rows, _ = blocks.shape
    parts = 4
    heads = count // micro // parts
    return pl.pallas_call(
        unpack_kernel,
        grid=(micro * parts,),
        in_specs=[pl.BlockSpec((heads, rows, 128), lambda i: (i, 0, 0))],
        out_specs=pl.BlockSpec((1, rows, heads * 128), lambda i: (i // parts, 0, i % parts)),
        out_shape=jax.ShapeDtypeStruct((micro, rows, parts * heads * 128), BF16),
        name="unpack",
        **PARAMS,
    )(blocks)


def items_of(positions):
    most = positions // CHUNK + DOCS - 1
    return (most + UNROLL - 1) // UNROLL * UNROLL


def work(positions, body):
    def some(i, carry):
        for u in range(UNROLL):
            body(i * UNROLL + u)
        return carry

    lax.fori_loop(0, items_of(positions) // UNROLL, some, 0)


def chunk_of(kv_ref, c):
    per = CHUNK // 128
    return kv_ref[0, pl.ds(c * per, per)].reshape(CHUNK, 128)


def lanes(d):
    return slice(d * TILE, (d + 1) * TILE)


def logits(product, c, first, last):
    position = lax.broadcasted_iota(jnp.int32, (CHUNK, TILE), 0) + c * CHUNK
    allowed = (position >= first) & (position < last)
    return jnp.where(allowed, product * LOG2, NEG)


def forward_items(plan_ref, kv_ref, query, lse, total, query_ref, top_ref, norm_ref, store):
    for d in range(DOCS):
        query_ref[d] = query[:, lanes(d)]
    query_ref[DOCS] = jnp.zeros((128, TILE), BF16)
    top_ref[...] = jnp.full(top_ref.shape, NEG, F32)
    norm_ref[...] = jnp.zeros(norm_ref.shape, F32)
    total[...] = jnp.zeros(total.shape, F32)
    positions = kv_ref.shape[1] * 128

    def stats(k):
        c, d = plan_ref[0, k], plan_ref[1, k]
        product = dot(chunk_of(kv_ref, c), query_ref[d], 1, 0)
        scores = logits(product, c, plan_ref[2, k], plan_ref[3, k])
        store[k] = scores
        groups = scores.reshape(CHUNK // 8, 8, TILE)
        top = jnp.max(groups, axis=0)
        norm = jnp.sum(jnp.exp2(groups - top[None]), axis=0)
        before = top_ref[d]
        now = jnp.maximum(before, top)
        norm_ref[d] = norm_ref[d] * jnp.exp2(before - now) + norm * jnp.exp2(top - now)
        top_ref[d] = now

    work(positions, stats)
    for d in range(DOCS + 1):
        top = top_ref[d]
        peak = jnp.max(top, axis=0, keepdims=True)
        norm = jnp.sum(norm_ref[d] * jnp.exp2(top - peak), axis=0, keepdims=True)
        lse[d] = jnp.broadcast_to(peak + jnp.log2(norm), (8, TILE))

    def gather(k):
        c, d = plan_ref[0, k], plan_ref[1, k]
        probs = jnp.exp2(store[k] - lse[d, 0:1])
        weights = probs.astype(BF16)
        left = (probs - weights.astype(F32)).astype(BF16)
        total[d] += dot(chunk_of(kv_ref, c), jnp.concatenate([weights, left], axis=1), 0, 0)

    work(positions, gather)


def forward_scratch(items):
    return [
        pltpu.VMEM((DOCS + 1, 128, 2 * TILE), F32),
        pltpu.VMEM((DOCS + 1, 128, TILE), BF16),
        pltpu.VMEM((DOCS + 1, 8, TILE), F32),
        pltpu.VMEM((DOCS + 1, 8, TILE), F32),
        pltpu.VMEM((items, CHUNK, TILE), F32),
    ]


def attended(total, d):
    attn = total[d, HEAD:, :TILE]
    return attn, attn + total[d, HEAD:, TILE:]


def pad_low(a):
    return jnp.concatenate([a, jnp.zeros_like(a)], axis=0)


def pad_high(a):
    return jnp.concatenate([jnp.zeros_like(a), a], axis=0)


def upright(a):
    return jnp.transpose(a.astype(F32)).astype(BF16)


def normed_query(xt, total, qgain):
    inv = lax.rsqrt(total / D + EPS)
    return inv, (xt * inv * qgain).astype(BF16)


def thirds(value):
    parts = []
    for _ in range(3):
        part = value.astype(BF16).astype(F32)
        parts.append(part)
        value = value - part
    return parts


def forward_kernel(
    plan_ref, kv_ref, tails_ref, xt_ref, place_ref, live_ref, qgain_ref, ogain_ref,
    out_ref, sums_ref, lse_ref, attn_ref, exact_ref, inv_ref,
    total_ref, query_ref, top_ref, norm_ref, store,
):
    tails = jnp.sum(tails_ref[...].astype(F32), axis=1)
    pieces = []
    for half in range(2):
        pieces += [
            tails[half, j : j + 1] + tails[half, j + 2 : j + 3] + tails[half, j + 4 : j + 5]
            for j in range(2)
        ]
    parts = thirds(jnp.concatenate(pieces, axis=1))
    parts.append(jnp.zeros((13, parts[0].shape[1]), F32))
    moved = dot(jnp.concatenate(parts, axis=0).astype(BF16), place_ref[...], 1, 0)
    total = jnp.sum(moved, axis=0, keepdims=True)
    xt = xt_ref[...].astype(F32)
    inv, query = normed_query(xt, total, qgain_ref[...])
    inv_ref[...] = inv
    forward_items(
        plan_ref, kv_ref, pad_low(query), lse_ref, total_ref, query_ref, top_ref, norm_ref, store
    )
    for d in range(DOCS):
        s = lanes(d)
        attn, exact = attended(total_ref, d)
        attn_ref[:, s] = attn
        exact_ref[:, s] = exact
        out = (xt[:, s] + ogain_ref[...] * attn) * live_ref[:, s]
        out_ref[:, s] = out.astype(BF16)
    out = out_ref[...].astype(F32)
    sums_ref[...] = jnp.broadcast_to(jnp.sum(out * out, axis=0, keepdims=True), sums_ref.shape)


def call(kernel, name, ins, outs, scratch, args, **more):
    return pl.pallas_call(
        kernel,
        grid=(1,),
        in_specs=ins,
        out_specs=[spec for spec, _ in outs],
        out_shape=[shape for _, shape in outs],
        scratch_shapes=scratch,
        name=name,
        **more,
        **PARAMS,
    )(*args)


def plain(shape, dtype=F32):
    return whole(shape), jax.ShapeDtypeStruct(shape, dtype)


def forward(plan, received, xt, place, live, qgain, ogain):
    width = xt.shape[1]
    blocks = received.shape[1]
    ins = [
        SMEM,
        vmem((1, blocks, 128, 128), (0, 0, 0, 0)),
        vmem((2, blocks, TAIL, 128), (0, 0, 128 // TAIL, 0)),
        whole((HEAD, width)),
        whole(place.shape),
        whole((1, width)),
        whole((HEAD, 1)),
        whole((HEAD, 1)),
    ]
    outs = [
        plain((HEAD, width), BF16),
        plain((blocks, width)),
        plain((DOCS + 1, 8, TILE)),
        plain((HEAD, width)),
        plain((HEAD, width)),
        plain((1, width)),
    ]
    return call(
        forward_kernel, "forward", ins, outs, forward_scratch(items_of(blocks * 128)),
        (plan, received, received, xt, place, live, qgain, ogain),
    )


def backward_step(keyval, probs, grad_probs, delta, pair, grad_kv_ref, c):
    grad_scores = (probs * (grad_probs - delta)).astype(BF16)
    left = jnp.concatenate([grad_scores, probs.astype(BF16)], axis=1)
    per = CHUNK // 128
    held = grad_kv_ref[0, pl.ds(c * per, per)].reshape(CHUNK, 128)
    added = held.astype(F32) + dot(left, pair, 1, 0)
    grad_kv_ref[0, pl.ds(c * per, per)] = added.astype(BF16).reshape(per, 128, 128)
    return dot(keyval, grad_scores, 0, 0)[:HEAD]


def fill_pairs(pair_ref, delta_ref, query, grad_out, deltas):
    keys_side = upright(query.astype(F32) * SCALE)
    values_side = upright(grad_out)
    for d in range(DOCS):
        s = lanes(d)
        pair_ref[d] = jnp.concatenate([keys_side[s], values_side[s]], axis=0)
        delta_ref[d] = jnp.broadcast_to(deltas[:, s], (8, TILE))
    pair_ref[DOCS] = jnp.zeros((2 * TILE, 128), BF16)
    delta_ref[DOCS] = jnp.zeros((8, TILE), F32)


def backward_scratch():
    return [
        pltpu.VMEM((DOCS + 1, 2 * TILE, 128), BF16),
        pltpu.VMEM((DOCS + 1, 8, TILE), F32),
        pltpu.VMEM((DOCS + 1, HEAD, TILE), F32),
    ]


def lined_up(ref):
    return jnp.concatenate([ref[d] for d in range(DOCS)], axis=1)


def middle_kernel(
    plan_ref, kv_ref, sums_ref, xt_ref, live_ref, qgain_ref, ogain_ref, gt_ref,
    grad_kv_ref, out_ref, cross_ref, grad_norm_ref, inv_ref, grad_qg_ref, grad_og_ref,
    total_ref, query_ref, top_ref, norm_ref, store,
    pair_ref, delta_ref, grad_query_ref, lse_ref, grad_ref,
):
    grad_kv_ref[...] = jnp.zeros_like(grad_kv_ref)
    grad_query_ref[...] = jnp.zeros_like(grad_query_ref)
    total = jnp.sum(sums_ref[...], axis=0, keepdims=True)
    xt = xt_ref[...].astype(F32)
    inv, low = normed_query(xt, total, qgain_ref[...])
    inv_ref[...] = inv
    query = pad_low(low)
    grad = gt_ref[...].astype(F32)
    grad_low = (grad * ogain_ref[...]).astype(BF16)
    grad_out = pad_high(grad_low)
    for d in range(DOCS):
        grad_ref[d] = grad_out[:, lanes(d)]
    grad_ref[DOCS] = jnp.zeros((128, TILE), BF16)
    forward_items(
        plan_ref, kv_ref, query, lse_ref, total_ref, query_ref, top_ref, norm_ref, store
    )
    both = [attended(total_ref, d) for d in range(DOCS)]
    attn = jnp.concatenate([a for a, _ in both], axis=1)
    exact = jnp.concatenate([e for _, e in both], axis=1)
    deltas = jnp.sum(grad_low.astype(F32) * exact, axis=0, keepdims=True)
    fill_pairs(pair_ref, delta_ref, query, grad_out, deltas)

    def back(k):
        c, d = plan_ref[0, k], plan_ref[1, k]
        keyval = chunk_of(kv_ref, c)
        probs = jnp.exp2(store[k] - lse_ref[d, 0:1])
        grad_probs = dot(keyval, grad_ref[d], 1, 0)
        grad_query_ref[d] += backward_step(
            keyval, probs, grad_probs, delta_ref[d, 0:1], pair_ref[d], grad_kv_ref, c
        )

    work(kv_ref.shape[1] * 128, back)
    out_ref[...] = ((xt + ogain_ref[...] * attn) * live_ref[...]).astype(BF16)
    grad_query = lined_up(grad_query_ref) * SCALE
    grad_norm = grad_query * qgain_ref[...]
    grad_norm_ref[...] = grad_norm
    cross = jnp.sum(grad_norm * xt, axis=0, keepdims=True)
    cross_ref[...] = jnp.broadcast_to(cross, cross_ref.shape)
    grad_qg_ref[...] = jnp.sum(grad_query * (xt * inv), axis=1, keepdims=True)
    grad_og_ref[...] = jnp.sum(grad * attn, axis=1, keepdims=True)


def middle(plan, received, sums, xt, live, qgain, ogain, gt):
    width = xt.shape[1]
    blocks = received.shape[1]
    ins = [
        SMEM,
        vmem((1, blocks, 128, 128), (1, 0, 0, 0)),
        whole((blocks, width)),
        whole((HEAD, width)),
        whole((1, width)),
        whole((HEAD, 1)),
        whole((HEAD, 1)),
        whole((HEAD, width)),
    ]
    outs = [
        (
            vmem((1, blocks, 128, 128), (1, 0, 0, 0)),
            jax.ShapeDtypeStruct((2, blocks, 128, 128), BF16),
        ),
        plain((HEAD, width), BF16),
        plain((blocks, width)),
        plain((HEAD, width)),
        plain((1, width)),
        plain((HEAD, 1)),
        plain((HEAD, 1)),
    ]
    scratch = forward_scratch(items_of(blocks * 128)) + backward_scratch()
    scratch += [
        pltpu.VMEM((DOCS + 1, 8, TILE), F32),
        pltpu.VMEM((DOCS + 1, 128, TILE), BF16),
    ]
    return call(
        middle_kernel, "middle", ins, outs, scratch,
        (plan, received, sums, xt, live, qgain, ogain, gt),
    )


def backward_kernel(
    plan_ref, kv_ref, cross_ref, gt_ref, grad_norm_ref, xt1_ref, inv1_ref,
    xt_ref, inv_ref, lse_ref, attn_ref, exact_ref, qgain_ref, ogain_ref, held_ref,
    grad_kv_ref, grad_qg_ref, grad_og_ref, pair_ref, delta_ref, grad_query_ref, both_ref,
):
    del held_ref
    grad_kv_ref[...] = jnp.zeros_like(grad_kv_ref)
    grad_query_ref[...] = jnp.zeros_like(grad_query_ref)
    cross = jnp.sum(cross_ref[...], axis=0, keepdims=True)
    inv1 = inv1_ref[...]
    xt1 = xt1_ref[...].astype(F32)
    grad = gt_ref[...].astype(F32) + inv1 * grad_norm_ref[...]
    grad = (grad - xt1 * (inv1 * inv1 * inv1) * (cross / D)).astype(BF16).astype(F32)
    grad_low = (grad * ogain_ref[...]).astype(BF16)
    grad_out = pad_high(grad_low)
    grad_og_ref[...] = jnp.sum(grad * attn_ref[...], axis=1, keepdims=True)
    deltas = jnp.sum(grad_low.astype(F32) * exact_ref[...], axis=0, keepdims=True)
    normed = xt_ref[...].astype(F32) * inv_ref[...]
    query = pad_low((normed * qgain_ref[...]).astype(BF16))
    fill_pairs(pair_ref, delta_ref, query, grad_out, deltas)
    for d in range(DOCS):
        both_ref[d] = jnp.concatenate([query[:, lanes(d)], grad_out[:, lanes(d)]], axis=1)
    both_ref[DOCS] = jnp.zeros((128, 2 * TILE), BF16)

    def back(k):
        c, d = plan_ref[0, k], plan_ref[1, k]
        keyval = chunk_of(kv_ref, c)
        product = dot(keyval, both_ref[d], 1, 0)
        scores = logits(product[:, :TILE], c, plan_ref[2, k], plan_ref[3, k])
        probs = jnp.exp2(scores - lse_ref[d, 0:1])
        grad_query_ref[d] += backward_step(
            keyval, probs, product[:, TILE:], delta_ref[d, 0:1], pair_ref[d], grad_kv_ref, c
        )

    work(kv_ref.shape[1] * 128, back)
    grad_query = lined_up(grad_query_ref) * SCALE
    grad_qg_ref[...] = jnp.sum(grad_query * normed, axis=1, keepdims=True)


def backward(
    plan, received, cross, gt, grad_norm, xt1, inv1, xt, inv, lse, attn, exact, qgain, ogain, held
):
    width = xt.shape[1]
    blocks = received.shape[1]
    ins = [
        SMEM,
        vmem((1, blocks, 128, 128), (0, 0, 0, 0)),
        whole((blocks, width)),
        whole((HEAD, width)),
        whole((HEAD, width)),
        whole((HEAD, width)),
        whole((1, width)),
        whole((HEAD, width)),
        whole((1, width)),
        whole(lse.shape),
        whole((HEAD, width)),
        whole((HEAD, width)),
        whole((HEAD, 1)),
        whole((HEAD, 1)),
        pl.BlockSpec(memory_space=pl.ANY),
    ]
    outs = [
        (
            vmem((1, blocks, 128, 128), (0, 0, 0, 0)),
            jax.ShapeDtypeStruct(held.shape, BF16),
        ),
        plain((HEAD, 1)),
        plain((HEAD, 1)),
    ]
    scratch = backward_scratch() + [pltpu.VMEM((DOCS + 1, 128, 2 * TILE), BF16)]
    return call(
        backward_kernel, "backward", ins, outs, scratch,
        (plan, received, cross, gt, grad_norm, xt1, inv1, xt, inv, lse, attn, exact,
         qgain, ogain, held),
        input_output_aliases={14: 0},
    )


def runs(seg):
    counts = [jnp.sum((seg < d).astype(jnp.int32)) for d in range(1, DOCS)]
    return jnp.stack([jnp.int32(0)] + counts + [jnp.int32(seg.shape[0])])


def plan_of(kseg):
    edges = runs(kseg)
    first, last = edges[:-1], edges[1:]
    start = first // CHUNK
    count = (last + (CHUNK - 1)) // CHUNK - start
    ends = jnp.cumsum(count)
    k = jnp.arange(items_of(kseg.shape[0]), dtype=jnp.int32)
    doc = jnp.sum((k[:, None] >= ends[None, :]).astype(jnp.int32), axis=1)
    chunk, low, high = jnp.zeros_like(k), jnp.zeros_like(k), jnp.full_like(k, kseg.shape[0])
    for d in range(DOCS):
        here = doc == d
        chunk = jnp.where(here, start[d] + k - (ends[d] - count[d]), chunk)
        low = jnp.where(here, first[d], low)
        high = jnp.where(here, last[d], high)
    return jnp.stack([chunk, doc, low, high])


def place_of(qseg):
    edges = runs(qseg)
    lane = jnp.arange(TILE, dtype=jnp.int32)
    row = (edges[:-1, None] + lane[None, :]).reshape(1, DOCS * TILE)
    live = (lane[None, :] < (edges[1:] - edges[:-1])[:, None]).reshape(1, DOCS * TILE)
    rows = jnp.arange(qseg.shape[0], dtype=jnp.int32)[:, None]
    return ((rows == row) & live).astype(BF16), live.astype(F32)


def placed(x, place):
    return lax.dot_general(
        x, place, (((0,), (0,)), ((), ())), preferred_element_type=F32
    ).astype(BF16)


def taken(xt, place):
    return lax.dot_general(
        place, xt, (((1,), (1,)), ((), ())), preferred_element_type=F32
    ).astype(BF16)


def swap(value):
    return lax.ppermute(value, "phase", [(0, 1), (1, 0)])


def spread(value):
    return lax.all_to_all(value, "seq", 0, 0, tiled=True)


def local(dec_in, enc_kv, dec_seg, enc_seg, q_gain, o_gain, cotangent):
    phase = lax.axis_index("phase")
    first_phase = phase == 0
    micro = dec_in.shape[0]
    positions = enc_seg.shape[1]
    blocks = positions // 128

    sent = pack(phase.reshape(1), enc_kv[0], dec_in)
    own = jnp.concatenate([q_gain, o_gain], axis=0)
    other = swap(own)
    received = lax.all_to_all(sent, BOTH, 0, 0, tiled=True)
    received = received.reshape(2, blocks, 128 + TAIL, 128)

    gains0 = jnp.where(first_phase, own, other)
    gains1 = jnp.where(first_phase, other, own)
    qgain0, ogain0 = gains0[0][:, None], gains0[1][:, None]
    qgain1, ogain1 = gains1[0][:, None], gains1[1][:, None]
    qseg = lax.dynamic_index_in_dim(dec_seg, phase, 0, keepdims=False)
    kseg = lax.dynamic_index_in_dim(enc_seg, phase, 0, keepdims=False)
    plan = plan_of(kseg)
    place, live = place_of(qseg)
    xt0 = placed(lax.dynamic_index_in_dim(dec_in, phase, 0, keepdims=False), place)
    gt = placed(lax.dynamic_index_in_dim(cotangent, phase, 0, keepdims=False), place)

    xt1, sums, lse0, attn0, exact0, inv0 = forward(
        plan, received, xt0, place, live, qgain0, ogain0
    )
    sums = spread(sums)
    grad_kv, xt2, cross, grad_norm, inv1, grad_qg1, grad_og1 = middle(
        plan, received, sums, xt1, live, qgain1, ogain1, gt
    )
    cross = spread(cross)
    grad_kv, grad_qg0, grad_og0 = backward(
        plan, received, cross, gt, grad_norm, xt1, inv1, xt0, inv0, lse0, attn0, exact0,
        qgain0, ogain0, grad_kv,
    )
    rows_back = lax.all_to_all(
        grad_kv.reshape(2 * blocks, 128, 128), BOTH, 0, 0, tiled=True
    )
    grad_rows = unpack(rows_back, micro)

    out0, out1 = taken(xt1, place), taken(xt2, place)
    mine = jnp.where(first_phase, out0, out1)
    theirs = swap(jnp.where(first_phase, out1, out0))
    sect_out = jnp.where(
        first_phase, jnp.stack([mine, theirs]), jnp.stack([theirs, mine])
    )
    grads0 = jnp.concatenate([grad_qg0, grad_og0], axis=1).T
    grads1 = jnp.concatenate([grad_qg1, grad_og1], axis=1).T
    grads = jnp.where(first_phase, grads0, grads1) + swap(
        jnp.where(first_phase, grads1, grads0)
    )
    return (sect_out[None], grad_rows[None], grads[0:1], grads[1:2])


def solution(mesh):
    in_specs = (
        P(None, None, "seq"),
        P("phase", None, "seq", None),
        P(),
        P(),
        P("phase", "seq"),
        P("phase", "seq"),
        P(None, None, "seq"),
    )
    out_specs = (
        P("phase", None, None, "seq"),
        P("phase", None, "seq", None),
        P("phase", "seq"),
        P("phase", "seq"),
    )
    return jax.shard_map(local, mesh=mesh, in_specs=in_specs, out_specs=out_specs, check_vma=False)
```

```python
import functools
import math

import jax
import jax.numpy as jnp
from jax import lax
from jax.experimental import pallas as pl
from jax.experimental.pallas import tpu as pltpu
from jax.sharding import PartitionSpec as P

D = 4096
HEAD = 64
EPS = 1e-06
NEG = -1e30
DOCS = 4
TILE = 256
CHUNK = 512
STEP1 = 10
STEP2 = 20
STEP3 = 5
GROUP = 8
VLIM = 60
TAIL = 16
SCALE = 1.0 / math.sqrt(HEAD)
LOG2 = SCALE * math.log2(math.e)
BOTH = ("phase", "seq")
F32 = jnp.float32
BF16 = jnp.bfloat16


def dot(a, b, ca, cb):
    return lax.dot_general(a, b, (((ca,), (cb,)), ((), ())), preferred_element_type=F32)


VMEM = pl.BlockSpec(memory_space=pltpu.VMEM)
SMEM = pl.BlockSpec(memory_space=pltpu.SMEM)
HBM = pl.BlockSpec(memory_space=pltpu.HBM)
PARAMS = dict(
    compiler_params=pltpu.CompilerParams(
        vmem_limit_bytes=VLIM * 1024 * 1024
    )
)


PIECES = 8


def pack_kernel(phase_ref, x_ref, kv_ref, out_ref, held, ready, in_sems, out_sems):
    per = out_ref.shape[0] // PIECES
    heads = kv_ref.shape[2] // 128
    arriving, leaving = [], []
    for i in range(PIECES):
        m, h = divmod(i * per, heads)
        source = kv_ref.at[m, :, pl.ds(h * 128, per * 128)]
        arriving.append(pltpu.make_async_copy(source, held.at[i], in_sems.at[i]))
        arriving[-1].start()
    tails = []
    for m in range(x_ref.shape[0]):
        half = pl.ds(pl.multiple_of(phase_ref[0] * 256, 256), 256)
        x = x_ref[m, :, half].astype(F32)
        rows = []
        for part in thirds(jnp.sum(x * x, axis=0, keepdims=True)):
            rows += [part[:, 0:128], part[:, 128:256]]
        rows.append(jnp.zeros((TAIL - 6, 128), F32))
        tails.append(jnp.concatenate(rows, axis=0).astype(BF16))
    for i in range(PIECES):
        arriving[i].wait()
        for j in range(per):
            ready[i * per + j, 0:128, :] = held[i, :, j * 128 : (j + 1) * 128]
            ready[i * per + j, 128 : 128 + TAIL, :] = tails[i * per // heads]
        piece = pl.ds(i * per, per)
        leaving.append(pltpu.make_async_copy(ready.at[piece], out_ref.at[piece], out_sems.at[i]))
        leaving[-1].start()
    for copy in leaving:
        copy.wait()


def pack(phase, kv, xts):
    micro, rows, feats = kv.shape
    count = micro * feats // 128
    shape = (count, rows + TAIL, 128)
    return pl.pallas_call(
        pack_kernel,
        in_specs=[SMEM, VMEM, HBM],
        out_specs=HBM,
        out_shape=jax.ShapeDtypeStruct(shape, BF16),
        scratch_shapes=[
            pltpu.VMEM((PIECES, rows, count // PIECES * 128), BF16),
            pltpu.VMEM(shape, BF16),
            pltpu.SemaphoreType.DMA((PIECES,)),
            pltpu.SemaphoreType.DMA((PIECES,)),
        ],
        name="pack",
        **PARAMS,
    )(phase, xts, kv)


def unpack_kernel(in_ref, out_ref, held, ready, in_sems, out_sems):
    per = in_ref.shape[0] // PIECES
    heads = out_ref.shape[2] // 128
    arriving, leaving = [], []
    for i in range(PIECES):
        piece = pl.ds(i * per, per)
        arriving.append(pltpu.make_async_copy(in_ref.at[piece], held.at[piece], in_sems.at[i]))
        arriving[-1].start()
    for i in range(PIECES):
        m, h = divmod(i * per, heads)
        arriving[i].wait()
        for j in range(per):
            ready[i, :, j * 128 : (j + 1) * 128] = held[i * per + j]
        target = out_ref.at[m, :, pl.ds(h * 128, per * 128)]
        leaving.append(pltpu.make_async_copy(ready.at[i], target, out_sems.at[i]))
        leaving[-1].start()
    for copy in leaving:
        copy.wait()


def unpack(blocks, micro):
    count, rows, _ = blocks.shape
    return pl.pallas_call(
        unpack_kernel,
        in_specs=[HBM],
        out_specs=HBM,
        out_shape=jax.ShapeDtypeStruct((micro, rows, count // micro * 128), BF16),
        scratch_shapes=[
            pltpu.VMEM(blocks.shape, BF16),
            pltpu.VMEM((PIECES, rows, count // PIECES * 128), BF16),
            pltpu.SemaphoreType.DMA((PIECES,)),
            pltpu.SemaphoreType.DMA((PIECES,)),
        ],
        name="unpack",
        **PARAMS,
    )(blocks)


def items_of(positions):
    return positions // CHUNK + DOCS


def fetches(received_ref, section, held, sems):
    copies = []
    for g in range(held.shape[0] // GROUP):
        piece = pl.ds(g * GROUP, GROUP)
        copies.append(
            pltpu.make_async_copy(
                received_ref.at[section, piece, pl.ds(0, 128), :], held.at[piece], sems.at[g]
            )
        )
        copies[-1].start()
    return copies


def work(kv_ref, body, step, before=None, after=None):
    items = items_of(kv_ref.shape[0] * 128)
    for start in range(0, items, step):
        stop = min(start + step, items)
        if before is not None:
            before(stop)
        for k in range(start, stop):
            body(k)
        if after is not None:
            after(stop, stop == items)


def halves(kv_ref, body, after):
    items = items_of(kv_ref.shape[0] * 128)
    step = items // 4

    def some(i, carry):
        for u in range(step):
            body(i * step + u)
        return carry

    lax.fori_loop(0, 2, some, 0)
    after(2 * step, False)
    lax.fori_loop(2, 4, some, 0)
    after(items, True)


def chunk_of(kv_ref, c):
    per = CHUNK // 128
    return kv_ref[pl.ds(c * per, per)].reshape(CHUNK, 128)


def lanes(d):
    return slice(d * TILE, (d + 1) * TILE)


def logits(product, c, first, last):
    position = lax.broadcasted_iota(jnp.int32, (CHUNK, TILE), 0) + c * CHUNK
    allowed = (position >= first) & (position < last)
    return jnp.where(allowed, product * LOG2, NEG)


def forward_items(plan_ref, kv_ref, copies, query, lse, total, query_ref, top_ref, norm_ref, store):
    for d in range(DOCS):
        query_ref[d] = query[:, lanes(d)]
    query_ref[DOCS] = jnp.zeros((128, TILE), BF16)
    top_ref[...] = jnp.full(top_ref.shape, NEG, F32)
    norm_ref[...] = jnp.zeros(norm_ref.shape, F32)
    total[...] = jnp.zeros(total.shape, F32)
    pending = list(copies)

    def stats(k):
        c, d = plan_ref[0, k], plan_ref[1, k]
        product = dot(chunk_of(kv_ref, c), query_ref[d], 1, 0)
        scores = logits(product, c, plan_ref[2, k], plan_ref[3, k])
        store[k] = scores
        groups = scores.reshape(CHUNK // 8, 8, TILE)
        top = jnp.max(groups, axis=0)
        norm = jnp.sum(jnp.exp2(groups - top[None]), axis=0)
        before = top_ref[d]
        now = jnp.maximum(before, top)
        norm_ref[d] = norm_ref[d] * jnp.exp2(before - now) + norm * jnp.exp2(top - now)
        top_ref[d] = now

    def arrived(stop):
        while pending and (len(copies) - len(pending)) * GROUP * 128 < stop * CHUNK:
            pending.pop(0).wait()

    work(kv_ref, stats, STEP1, before=arrived)
    for d in range(DOCS + 1):
        top = top_ref[d]
        peak = jnp.max(top, axis=0, keepdims=True)
        norm = jnp.sum(norm_ref[d] * jnp.exp2(top - peak), axis=0, keepdims=True)
        lse[d] = jnp.broadcast_to(peak + jnp.log2(norm), (8, TILE))

    def gather(k):
        c, d = plan_ref[0, k], plan_ref[1, k]
        probs = jnp.exp2(store[k] - lse[d, 0:1])
        weights = probs.astype(BF16)
        left = (probs - weights.astype(F32)).astype(BF16)
        total[d] += dot(chunk_of(kv_ref, c), jnp.concatenate([weights, left], axis=1), 0, 0)

    work(kv_ref, gather, STEP2)


def kv_scratch(blocks):
    return [
        pltpu.VMEM((blocks, 128, 128), BF16),
        pltpu.SemaphoreType.DMA((blocks // GROUP,)),
    ]


def forward_scratch(blocks):
    return [
        pltpu.VMEM((DOCS + 1, 128, 2 * TILE), F32),
        pltpu.VMEM((DOCS + 1, 128, TILE), BF16),
        pltpu.VMEM((DOCS + 1, 8, TILE), F32),
        pltpu.VMEM((DOCS + 1, 8, TILE), F32),
        pltpu.VMEM((items_of(blocks * 128), CHUNK, TILE), F32),
    ]


def attended(total, d):
    attn = total[d, HEAD:, :TILE]
    return attn, attn + total[d, HEAD:, TILE:]


def pad_low(a):
    return jnp.concatenate([a, jnp.zeros_like(a)], axis=0)


def pad_high(a):
    return jnp.concatenate([jnp.zeros_like(a), a], axis=0)


def upright(a):
    return jnp.transpose(a.astype(F32)).astype(BF16)


def normed_query(xt, total, qgain):
    inv = lax.rsqrt(total / D + EPS)
    return inv, (xt * inv * qgain).astype(BF16)


def as_messages(row, shape):
    tile = jnp.concatenate([row[:, 128 * j : 128 * j + 128] for j in range(shape[1])], axis=0)
    return jnp.broadcast_to(tile[None], shape)


def total_of(ref):
    tile = jnp.sum(ref[...], axis=0)
    return jnp.concatenate([tile[j : j + 1] for j in range(tile.shape[0])], axis=1)


def thirds(value):
    parts = []
    for _ in range(3):
        part = value.astype(BF16).astype(F32)
        parts.append(part)
        value = value - part
    return parts


def forward_kernel(
    plan_ref, xt_ref, row_ref, qgain_ref, ogain_ref, received_ref,
    out_ref, sums_ref, lse_ref, attn_ref, exact_ref, inv_ref,
    total_ref, query_ref, top_ref, norm_ref, store, kv_ref, sems, tails_ref, tails_sem,
):
    tails_copy = pltpu.make_async_copy(
        received_ref.at[:, :, pl.ds(128, TAIL), :], tails_ref, tails_sem
    )
    tails_copy.start()
    copies = fetches(received_ref, 0, kv_ref, sems)
    tails_copy.wait()
    tails = jnp.sum(tails_ref[...].astype(F32), axis=1)
    pieces = []
    for half in range(2):
        pieces += [
            tails[half, j : j + 1] + tails[half, j + 2 : j + 3] + tails[half, j + 4 : j + 5]
            for j in range(2)
        ]
    parts = thirds(jnp.concatenate(pieces, axis=1))
    parts.append(jnp.zeros((13, parts[0].shape[1]), F32))
    row = row_ref[...]
    rows = lax.broadcasted_iota(jnp.int32, (parts[0].shape[1], row.shape[1]), 0)
    place = jnp.where(rows == row, 1.0, 0.0).astype(BF16)
    moved = dot(jnp.concatenate(parts, axis=0).astype(BF16), place, 1, 0)
    total = jnp.sum(moved, axis=0, keepdims=True)
    xt = xt_ref[...].astype(F32)
    inv, query = normed_query(xt, total, qgain_ref[...])
    inv_ref[...] = inv
    forward_items(
        plan_ref, kv_ref, copies, pad_low(query), lse_ref, total_ref, query_ref, top_ref, norm_ref, store
    )
    for d in range(DOCS):
        s = lanes(d)
        attn, exact = attended(total_ref, d)
        attn_ref[:, s] = attn
        exact_ref[:, s] = exact
        out = xt[:, s] + ogain_ref[...] * attn
        out_ref[:, s] = jnp.where(row[:, s] >= 0, out, 0.0).astype(BF16)
    out = out_ref[...].astype(F32)
    sums_ref[...] = as_messages(jnp.sum(out * out, axis=0, keepdims=True), sums_ref.shape)


def call(kernel, name, ins, outs, scratch, args, **more):
    return pl.pallas_call(
        kernel,
        in_specs=ins,
        out_specs=[spec for spec, _ in outs],
        out_shape=[shape for _, shape in outs],
        scratch_shapes=scratch,
        name=name,
        **more,
        **PARAMS,
    )(*args)


def plain(shape, dtype=F32):
    return VMEM, jax.ShapeDtypeStruct(shape, dtype)


def forward(plan, received, xt, row, qgain, ogain):
    width = xt.shape[1]
    blocks = received.shape[1]
    outs = [
        plain((HEAD, width), BF16),
        plain((blocks, width // 128, 128)),
        plain((DOCS + 1, 8, TILE)),
        plain((HEAD, width)),
        plain((HEAD, width)),
        plain((1, width)),
    ]
    scratch = forward_scratch(blocks) + kv_scratch(blocks)
    scratch += [pltpu.VMEM((2, blocks, TAIL, 128), BF16), pltpu.SemaphoreType.DMA]
    return call(
        forward_kernel, "forward", [SMEM] + [VMEM] * 4 + [HBM], outs, scratch,
        (plan, xt, row, qgain, ogain, received),
    )


def backward_step(keyval, probs, grad_probs, delta, pair, grad_kv_ref, c):
    grad_scores = (probs * (grad_probs - delta)).astype(BF16)
    left = jnp.concatenate([grad_scores, probs.astype(BF16)], axis=1)
    per = CHUNK // 128
    held = grad_kv_ref[pl.ds(c * per, per)].reshape(CHUNK, 128)
    added = held.astype(F32) + dot(left, pair, 1, 0)
    grad_kv_ref[pl.ds(c * per, per)] = added.astype(BF16).reshape(per, 128, 128)
    return dot(keyval, grad_scores, 0, 0)[:HEAD]


class Leaving:
    def __init__(self, held, out_ref, section, sems):
        self.copies = []
        self.parts = (held, out_ref, section, sems)

    def after(self, stop, last):
        held, out_ref, section, sems = self.parts
        blocks = held.shape[0]
        done = blocks if last else max(0, stop - (DOCS - 1)) * (CHUNK // 128)
        while (len(self.copies) + 1) * GROUP <= done:
            g = len(self.copies)
            piece = pl.ds(g * GROUP, GROUP)
            copy = pltpu.make_async_copy(held.at[piece], out_ref.at[section, piece], sems.at[g])
            copy.start()
            self.copies.append(copy)

    def wait(self):
        for copy in self.copies:
            copy.wait()


def fill_pairs(pair_ref, delta_ref, query, grad_out, deltas):
    keys_side = upright(query.astype(F32) * SCALE)
    values_side = upright(grad_out)
    for d in range(DOCS):
        s = lanes(d)
        pair_ref[d] = jnp.concatenate([keys_side[s], values_side[s]], axis=0)
        delta_ref[d] = jnp.broadcast_to(deltas[:, s], (8, TILE))
    pair_ref[DOCS] = jnp.zeros((2 * TILE, 128), BF16)
    delta_ref[DOCS] = jnp.zeros((8, TILE), F32)


def backward_scratch():
    return [
        pltpu.VMEM((DOCS + 1, 2 * TILE, 128), BF16),
        pltpu.VMEM((DOCS + 1, 8, TILE), F32),
        pltpu.VMEM((DOCS + 1, HEAD, TILE), F32),
    ]


def lined_up(ref):
    return jnp.concatenate([ref[d] for d in range(DOCS)], axis=1)


def middle_kernel(
    plan_ref, sums_ref, xt_ref, qgain_ref, ogain_ref, gt_ref, received_ref,
    result_ref, out_ref, cross_ref, grad_norm_ref, inv_ref, grad_qg_ref, grad_og_ref,
    total_ref, query_ref, top_ref, norm_ref, store,
    pair_ref, delta_ref, grad_query_ref, lse_ref, grad_ref,
    kv_ref, sems, grad_kv_ref, out_sems,
):
    copies = fetches(received_ref, 1, kv_ref, sems)
    grad_kv_ref[...] = jnp.zeros_like(grad_kv_ref)
    grad_query_ref[...] = jnp.zeros_like(grad_query_ref)
    total = total_of(sums_ref)
    xt = xt_ref[...].astype(F32)
    inv, low = normed_query(xt, total, qgain_ref[...])
    inv_ref[...] = inv
    query = pad_low(low)
    grad = gt_ref[...].astype(F32)
    grad_low = (grad * ogain_ref[...]).astype(BF16)
    grad_out = pad_high(grad_low)
    for d in range(DOCS):
        grad_ref[d] = grad_out[:, lanes(d)]
    grad_ref[DOCS] = jnp.zeros((128, TILE), BF16)
    forward_items(
        plan_ref, kv_ref, copies, query, lse_ref, total_ref, query_ref, top_ref, norm_ref, store
    )
    both = [attended(total_ref, d) for d in range(DOCS)]
    attn = jnp.concatenate([a for a, _ in both], axis=1)
    exact = jnp.concatenate([e for _, e in both], axis=1)
    deltas = jnp.sum(grad_low.astype(F32) * exact, axis=0, keepdims=True)
    fill_pairs(pair_ref, delta_ref, query, grad_out, deltas)

    def back(k):
        c, d = plan_ref[0, k], plan_ref[1, k]
        keyval = chunk_of(kv_ref, c)
        probs = jnp.exp2(store[k] - lse_ref[d, 0:1])
        grad_probs = dot(keyval, grad_ref[d], 1, 0)
        grad_query_ref[d] += backward_step(
            keyval, probs, grad_probs, delta_ref[d, 0:1], pair_ref[d], grad_kv_ref, c
        )

    leaving = Leaving(grad_kv_ref, result_ref, 1, out_sems)
    halves(kv_ref, back, leaving.after)
    out_ref[...] = (xt + ogain_ref[...] * attn).astype(BF16)
    grad_query = lined_up(grad_query_ref) * SCALE
    grad_norm = grad_query * qgain_ref[...]
    grad_norm_ref[...] = grad_norm
    cross = jnp.sum(grad_norm * xt, axis=0, keepdims=True)
    cross_ref[...] = as_messages(cross, cross_ref.shape)
    grad_qg_ref[...] = jnp.sum(grad_query * (xt * inv), axis=1, keepdims=True)
    grad_og_ref[...] = jnp.sum(grad * attn, axis=1, keepdims=True)
    leaving.wait()


def middle(plan, received, sums, xt, qgain, ogain, gt):
    width = xt.shape[1]
    blocks = received.shape[1]
    outs = [
        (HBM, jax.ShapeDtypeStruct((2, blocks, 128, 128), BF16)),
        plain((HEAD, width), BF16),
        plain((blocks, width // 128, 128)),
        plain((HEAD, width)),
        plain((1, width)),
        plain((HEAD, 1)),
        plain((HEAD, 1)),
    ]
    scratch = forward_scratch(blocks) + backward_scratch()
    scratch += [
        pltpu.VMEM((DOCS + 1, 8, TILE), F32),
        pltpu.VMEM((DOCS + 1, 128, TILE), BF16),
    ]
    scratch += kv_scratch(blocks) + kv_scratch(blocks)
    return call(
        middle_kernel, "middle", [SMEM] + [VMEM] * 5 + [HBM], outs, scratch,
        (plan, sums, xt, qgain, ogain, gt, received),
    )


def backward_kernel(
    plan_ref, cross_ref, gt_ref, grad_norm_ref, xt1_ref, inv1_ref,
    xt_ref, inv_ref, lse_ref, attn_ref, exact_ref, qgain_ref, ogain_ref, received_ref, begun_ref,
    result_ref, grad_qg_ref, grad_og_ref, pair_ref, delta_ref, grad_query_ref, both_ref,
    kv_ref, sems, grad_kv_ref, out_sems,
):
    del begun_ref
    copies = fetches(received_ref, 0, kv_ref, sems)
    grad_kv_ref[...] = jnp.zeros_like(grad_kv_ref)
    grad_query_ref[...] = jnp.zeros_like(grad_query_ref)
    cross = total_of(cross_ref)
    inv1 = inv1_ref[...]
    xt1 = xt1_ref[...].astype(F32)
    grad = gt_ref[...].astype(F32) + inv1 * grad_norm_ref[...]
    grad = (grad - xt1 * (inv1 * inv1 * inv1) * (cross / D)).astype(BF16).astype(F32)
    grad_low = (grad * ogain_ref[...]).astype(BF16)
    grad_out = pad_high(grad_low)
    grad_og_ref[...] = jnp.sum(grad * attn_ref[...], axis=1, keepdims=True)
    deltas = jnp.sum(grad_low.astype(F32) * exact_ref[...], axis=0, keepdims=True)
    normed = xt_ref[...].astype(F32) * inv_ref[...]
    query = pad_low((normed * qgain_ref[...]).astype(BF16))
    fill_pairs(pair_ref, delta_ref, query, grad_out, deltas)
    for d in range(DOCS):
        both_ref[d] = jnp.concatenate([query[:, lanes(d)], grad_out[:, lanes(d)]], axis=1)
    both_ref[DOCS] = jnp.zeros((128, 2 * TILE), BF16)

    def back(k):
        c, d = plan_ref[0, k], plan_ref[1, k]
        keyval = chunk_of(kv_ref, c)
        product = dot(keyval, both_ref[d], 1, 0)
        scores = logits(product[:, :TILE], c, plan_ref[2, k], plan_ref[3, k])
        probs = jnp.exp2(scores - lse_ref[d, 0:1])
        grad_query_ref[d] += backward_step(
            keyval, probs, product[:, TILE:], delta_ref[d, 0:1], pair_ref[d], grad_kv_ref, c
        )

    for copy in copies:
        copy.wait()
    leaving = Leaving(grad_kv_ref, result_ref, 0, out_sems)
    halves(kv_ref, back, leaving.after)
    grad_query = lined_up(grad_query_ref) * SCALE
    grad_qg_ref[...] = jnp.sum(grad_query * normed, axis=1, keepdims=True)
    leaving.wait()


def backward(
    plan, received, cross, gt, grad_norm, xt1, inv1, xt, inv, lse, attn, exact, qgain, ogain, begun
):
    blocks = received.shape[1]
    outs = [
        (HBM, jax.ShapeDtypeStruct(begun.shape, BF16)),
        plain((HEAD, 1)),
        plain((HEAD, 1)),
    ]
    scratch = backward_scratch() + [pltpu.VMEM((DOCS + 1, 128, 2 * TILE), BF16)]
    scratch += kv_scratch(blocks) + kv_scratch(blocks)
    return call(
        backward_kernel, "backward", [SMEM] + [VMEM] * 12 + [HBM] * 2, outs, scratch,
        (plan, cross, gt, grad_norm, xt1, inv1, xt, inv, lse, attn, exact,
         qgain, ogain, received, begun),
        input_output_aliases={14: 0},
    )


def runs(seg):
    counts = [jnp.sum((seg < d).astype(jnp.int32)) for d in range(1, DOCS)]
    return jnp.stack([jnp.int32(0)] + counts + [jnp.int32(seg.shape[0])])


def plan_of(kseg):
    edges = runs(kseg)
    first, last = edges[:-1], edges[1:]
    start = first // CHUNK
    count = (last + (CHUNK - 1)) // CHUNK - start
    ends = jnp.cumsum(count)
    k = jnp.arange(items_of(kseg.shape[0]), dtype=jnp.int32)
    doc = jnp.sum((k[:, None] >= ends[None, :]).astype(jnp.int32), axis=1)
    chunk = jnp.full_like(k, kseg.shape[0] // CHUNK - 1)
    low, high = jnp.zeros_like(k), jnp.full_like(k, kseg.shape[0])
    for d in range(DOCS):
        here = doc == d
        chunk = jnp.where(here, start[d] + k - (ends[d] - count[d]), chunk)
        low = jnp.where(here, first[d], low)
        high = jnp.where(here, last[d], high)
    return jnp.stack([chunk, doc, low, high])


def place_of(qseg):
    edges = runs(qseg)
    lane = jnp.arange(TILE, dtype=jnp.int32)
    row = (edges[:-1, None] + lane[None, :]).reshape(1, DOCS * TILE)
    live = (lane[None, :] < (edges[1:] - edges[:-1])[:, None]).reshape(1, DOCS * TILE)
    rows = jnp.arange(qseg.shape[0], dtype=jnp.int32)[:, None]
    row = jnp.where(live, row, -1)
    return (rows == row).astype(BF16), row


def placed(x, place):
    return lax.dot_general(
        x, place, (((0,), (0,)), ((), ())), preferred_element_type=F32
    ).astype(BF16)


def taken(xt, place):
    return lax.dot_general(
        place, xt, (((1,), (1,)), ((), ())), preferred_element_type=F32
    ).astype(BF16)


def swap(value):
    return lax.ppermute(value, "phase", [(0, 1), (1, 0)])


def spread(value):
    return lax.all_to_all(value, "seq", 0, 0, tiled=True)


def local(dec_in, enc_kv, dec_seg, enc_seg, q_gain, o_gain, cotangent):
    phase = lax.axis_index("phase")
    first_phase = phase == 0
    micro = dec_in.shape[0]
    positions = enc_seg.shape[1]
    blocks = positions // 128

    sent = pack(phase.reshape(1), enc_kv[0], jnp.transpose(dec_in, (0, 2, 1)))
    own = jnp.concatenate([q_gain, o_gain], axis=0)
    other = swap(own)
    received = lax.all_to_all(sent, BOTH, 0, 0, tiled=True)
    received = received.reshape(2, blocks, 128 + TAIL, 128)

    gains0 = jnp.where(first_phase, own, other)
    gains1 = jnp.where(first_phase, other, own)
    qgain0, ogain0 = gains0[0][:, None], gains0[1][:, None]
    qgain1, ogain1 = gains1[0][:, None], gains1[1][:, None]
    qseg = lax.dynamic_index_in_dim(dec_seg, phase, 0, keepdims=False)
    kseg = lax.dynamic_index_in_dim(enc_seg, phase, 0, keepdims=False)
    plan = plan_of(kseg)
    place, row = place_of(qseg)
    xt0 = placed(lax.dynamic_index_in_dim(dec_in, phase, 0, keepdims=False), place)
    gt = placed(lax.dynamic_index_in_dim(cotangent, phase, 0, keepdims=False), place)

    xt1, sums, lse0, attn0, exact0, inv0 = forward(
        plan, received, xt0, row, qgain0, ogain0
    )
    sums = spread(sums)
    grad_kv, xt2, cross, grad_norm, inv1, grad_qg1, grad_og1 = middle(
        plan, received, sums, xt1, qgain1, ogain1, gt
    )
    cross = spread(cross)
    grad_kv, grad_qg0, grad_og0 = backward(
        plan, received, cross, gt, grad_norm, xt1, inv1, xt0, inv0, lse0, attn0, exact0,
        qgain0, ogain0, grad_kv,
    )
    rows_back = lax.all_to_all(
        grad_kv.reshape(2 * blocks, 128, 128), BOTH, 0, 0, tiled=True
    )
    grad_rows = unpack(rows_back, micro)

    out0, out1 = taken(xt1, place), taken(xt2, place)
    mine = jnp.where(first_phase, out0, out1)
    theirs = swap(jnp.where(first_phase, out1, out0))
    sect_out = jnp.where(
        first_phase, jnp.stack([mine, theirs]), jnp.stack([theirs, mine])
    )
    grads0 = jnp.concatenate([grad_qg0, grad_og0], axis=1).T
    grads1 = jnp.concatenate([grad_qg1, grad_og1], axis=1).T
    grads = jnp.where(first_phase, grads0, grads1) + swap(
        jnp.where(first_phase, grads1, grads0)
    )
    return (sect_out[None], grad_rows[None], grads[0:1], grads[1:2])


def solution(mesh):
    in_specs = (
        P(None, None, "seq"),
        P("phase", None, "seq", None),
        P(),
        P(),
        P("phase", "seq"),
        P("phase", "seq"),
        P(None, None, "seq"),
    )
    out_specs = (
        P("phase", None, None, "seq"),
        P("phase", None, "seq", None),
        P("phase", "seq"),
        P("phase", "seq"),
    )
    return jax.shard_map(local, mesh=mesh, in_specs=in_specs, out_specs=out_specs, check_vma=False)
```

```python
import functools
import math

import jax
import jax.numpy as jnp
from jax import lax
from jax.experimental import pallas as pl
from jax.experimental.pallas import tpu as pltpu
from jax.sharding import PartitionSpec as P

D = 4096
HEAD = 64
EPS = 1e-06
NEG = -1e30
DOCS = 4
TILE = 256
CHUNK = 512
UNROLL = 10
TAIL = 16
SCALE = 1.0 / math.sqrt(HEAD)
LOG2 = SCALE * math.log2(math.e)
BOTH = ("phase", "seq")
F32 = jnp.float32
BF16 = jnp.bfloat16


def dot(a, b, ca, cb):
    return lax.dot_general(a, b, (((ca,), (cb,)), ((), ())), preferred_element_type=F32)


def vmem(shape, index):
    return pl.BlockSpec(shape, lambda i: index)


def whole(shape):
    return vmem(shape, (0,) * len(shape))


SMEM = pl.BlockSpec(memory_space=pltpu.SMEM)
PARAMS = dict(
    compiler_params=pltpu.CompilerParams(
        dimension_semantics=("arbitrary",), vmem_limit_bytes=60 * 1024 * 1024
    )
)
SIMPLE = dict(compiler_params=pltpu.CompilerParams(vmem_limit_bytes=60 * 1024 * 1024))
HBM = pl.BlockSpec(memory_space=pltpu.HBM)
VMEM = pl.BlockSpec(memory_space=pltpu.VMEM)


PIECES = 8


def pack_kernel(phase_ref, x_ref, kv_ref, out_ref, held, ready, in_sems, out_sems):
    per = out_ref.shape[0] // PIECES
    heads = kv_ref.shape[2] // 128
    arriving, leaving = [], []
    for i in range(PIECES):
        m, h = divmod(i * per, heads)
        source = kv_ref.at[m, :, pl.ds(h * 128, per * 128)]
        arriving.append(pltpu.make_async_copy(source, held.at[i], in_sems.at[i]))
        arriving[-1].start()
    tails = []
    for m in range(x_ref.shape[0]):
        half = pl.ds(pl.multiple_of(phase_ref[0] * 256, 256), 256)
        x = x_ref[m, :, half].astype(F32)
        rows = []
        for part in thirds(jnp.sum(x * x, axis=0, keepdims=True)):
            rows += [part[:, 0:128], part[:, 128:256]]
        rows.append(jnp.zeros((TAIL - 6, 128), F32))
        tails.append(jnp.concatenate(rows, axis=0).astype(BF16))
    for i in range(PIECES):
        arriving[i].wait()
        for j in range(per):
            ready[i * per + j, 0:128, :] = held[i, :, j * 128 : (j + 1) * 128]
            ready[i * per + j, 128 : 128 + TAIL, :] = tails[i * per // heads]
        piece = pl.ds(i * per, per)
        leaving.append(pltpu.make_async_copy(ready.at[piece], out_ref.at[piece], out_sems.at[i]))
        leaving[-1].start()
    for copy in leaving:
        copy.wait()


def pack(phase, kv, xts):
    micro, rows, feats = kv.shape
    count = micro * feats // 128
    shape = (count, rows + TAIL, 128)
    return pl.pallas_call(
        pack_kernel,
        in_specs=[SMEM, VMEM, HBM],
        out_specs=HBM,
        out_shape=jax.ShapeDtypeStruct(shape, BF16),
        scratch_shapes=[
            pltpu.VMEM((PIECES, rows, count // PIECES * 128), BF16),
            pltpu.VMEM(shape, BF16),
            pltpu.SemaphoreType.DMA((PIECES,)),
            pltpu.SemaphoreType.DMA((PIECES,)),
        ],
        name="pack",
        **SIMPLE,
    )(phase, xts, kv)


def unpack_kernel(in_ref, out_ref, held, ready, in_sems, out_sems):
    per = in_ref.shape[0] // PIECES
    heads = out_ref.shape[2] // 128
    arriving, leaving = [], []
    for i in range(PIECES):
        piece = pl.ds(i * per, per)
        arriving.append(pltpu.make_async_copy(in_ref.at[piece], held.at[piece], in_sems.at[i]))
        arriving[-1].start()
    for i in range(PIECES):
        m, h = divmod(i * per, heads)
        arriving[i].wait()
        for j in range(per):
            ready[i, :, j * 128 : (j + 1) * 128] = held[i * per + j]
        target = out_ref.at[m, :, pl.ds(h * 128, per * 128)]
        leaving.append(pltpu.make_async_copy(ready.at[i], target, out_sems.at[i]))
        leaving[-1].start()
    for copy in leaving:
        copy.wait()


def unpack(blocks, micro):
    count, rows, _ = blocks.shape
    return pl.pallas_call(
        unpack_kernel,
        in_specs=[HBM],
        out_specs=HBM,
        out_shape=jax.ShapeDtypeStruct((micro, rows, count // micro * 128), BF16),
        scratch_shapes=[
            pltpu.VMEM(blocks.shape, BF16),
            pltpu.VMEM((PIECES, rows, count // PIECES * 128), BF16),
            pltpu.SemaphoreType.DMA((PIECES,)),
            pltpu.SemaphoreType.DMA((PIECES,)),
        ],
        name="unpack",
        **SIMPLE,
    )(blocks)


def items_of(positions):
    most = positions // CHUNK + DOCS - 1
    return (most + UNROLL - 1) // UNROLL * UNROLL


def work(positions, body):
    def some(i, carry):
        for u in range(UNROLL):
            body(i * UNROLL + u)
        return carry

    lax.fori_loop(0, items_of(positions) // UNROLL, some, 0)


def chunk_of(kv_ref, c):
    per = CHUNK // 128
    return kv_ref[0, pl.ds(c * per, per)].reshape(CHUNK, 128)


def lanes(d):
    return slice(d * TILE, (d + 1) * TILE)


def logits(product, c, first, last):
    position = lax.broadcasted_iota(jnp.int32, (CHUNK, TILE), 0) + c * CHUNK
    allowed = (position >= first) & (position < last)
    return jnp.where(allowed, product * LOG2, NEG)


def forward_items(plan_ref, kv_ref, query, lse, total, query_ref, top_ref, norm_ref, store):
    for d in range(DOCS):
        query_ref[d] = query[:, lanes(d)]
    query_ref[DOCS] = jnp.zeros((128, TILE), BF16)
    top_ref[...] = jnp.full(top_ref.shape, NEG, F32)
    norm_ref[...] = jnp.zeros(norm_ref.shape, F32)
    total[...] = jnp.zeros(total.shape, F32)
    positions = kv_ref.shape[1] * 128

    def stats(k):
        c, d = plan_ref[0, k], plan_ref[1, k]
        product = dot(chunk_of(kv_ref, c), query_ref[d], 1, 0)
        scores = logits(product, c, plan_ref[2, k], plan_ref[3, k])
        store[k] = scores
        groups = scores.reshape(CHUNK // 8, 8, TILE)
        top = jnp.max(groups, axis=0)
        norm = jnp.sum(jnp.exp2(groups - top[None]), axis=0)
        before = top_ref[d]
        now = jnp.maximum(before, top)
        norm_ref[d] = norm_ref[d] * jnp.exp2(before - now) + norm * jnp.exp2(top - now)
        top_ref[d] = now

    work(positions, stats)
    for d in range(DOCS + 1):
        top = top_ref[d]
        peak = jnp.max(top, axis=0, keepdims=True)
        norm = jnp.sum(norm_ref[d] * jnp.exp2(top - peak), axis=0, keepdims=True)
        lse[d] = jnp.broadcast_to(peak + jnp.log2(norm), (8, TILE))

    def gather(k):
        c, d = plan_ref[0, k], plan_ref[1, k]
        probs = jnp.exp2(store[k] - lse[d, 0:1])
        weights = probs.astype(BF16)
        left = (probs - weights.astype(F32)).astype(BF16)
        total[d] += dot(chunk_of(kv_ref, c), jnp.concatenate([weights, left], axis=1), 0, 0)

    work(positions, gather)


def forward_scratch(items):
    return [
        pltpu.VMEM((DOCS + 1, 128, 2 * TILE), F32),
        pltpu.VMEM((DOCS + 1, 128, TILE), BF16),
        pltpu.VMEM((DOCS + 1, 8, TILE), F32),
        pltpu.VMEM((DOCS + 1, 8, TILE), F32),
        pltpu.VMEM((items, CHUNK, TILE), F32),
    ]


def attended(total, d):
    attn = total[d, HEAD:, :TILE]
    return attn, attn + total[d, HEAD:, TILE:]


def pad_low(a):
    return jnp.concatenate([a, jnp.zeros_like(a)], axis=0)


def pad_high(a):
    return jnp.concatenate([jnp.zeros_like(a), a], axis=0)


def upright(a):
    return jnp.transpose(a.astype(F32)).astype(BF16)


def normed_query(xt, total, qgain):
    inv = lax.rsqrt(total / D + EPS)
    return inv, (xt * inv * qgain).astype(BF16)


def as_messages(row, shape):
    tile = jnp.concatenate([row[:, 128 * j : 128 * j + 128] for j in range(shape[1])], axis=0)
    return jnp.broadcast_to(tile[None], shape)


def total_of(ref):
    tile = jnp.sum(ref[...], axis=0)
    return jnp.concatenate([tile[j : j + 1] for j in range(tile.shape[0])], axis=1)


def thirds(value):
    parts = []
    for _ in range(3):
        part = value.astype(BF16).astype(F32)
        parts.append(part)
        value = value - part
    return parts


def forward_kernel(
    plan_ref, kv_ref, tails_ref, xt_ref, place_ref, live_ref, qgain_ref, ogain_ref,
    out_ref, sums_ref, lse_ref, attn_ref, exact_ref, inv_ref,
    total_ref, query_ref, top_ref, norm_ref, store,
):
    tails = jnp.sum(tails_ref[...].astype(F32), axis=1)
    pieces = []
    for half in range(2):
        pieces += [
            tails[half, j : j + 1] + tails[half, j + 2 : j + 3] + tails[half, j + 4 : j + 5]
            for j in range(2)
        ]
    parts = thirds(jnp.concatenate(pieces, axis=1))
    parts.append(jnp.zeros((13, parts[0].shape[1]), F32))
    moved = dot(jnp.concatenate(parts, axis=0).astype(BF16), place_ref[...], 1, 0)
    total = jnp.sum(moved, axis=0, keepdims=True)
    xt = xt_ref[...].astype(F32)
    inv, query = normed_query(xt, total, qgain_ref[...])
    inv_ref[...] = inv
    forward_items(
        plan_ref, kv_ref, pad_low(query), lse_ref, total_ref, query_ref, top_ref, norm_ref, store
    )
    for d in range(DOCS):
        s = lanes(d)
        attn, exact = attended(total_ref, d)
        attn_ref[:, s] = attn
        exact_ref[:, s] = exact
        out = (xt[:, s] + ogain_ref[...] * attn) * live_ref[:, s]
        out_ref[:, s] = out.astype(BF16)
    out = out_ref[...].astype(F32)
    sums_ref[...] = as_messages(jnp.sum(out * out, axis=0, keepdims=True), sums_ref.shape)


def call(kernel, name, ins, outs, scratch, args, **more):
    return pl.pallas_call(
        kernel,
        grid=(1,),
        in_specs=ins,
        out_specs=[spec for spec, _ in outs],
        out_shape=[shape for _, shape in outs],
        scratch_shapes=scratch,
        name=name,
        **more,
        **PARAMS,
    )(*args)


def plain(shape, dtype=F32):
    return whole(shape), jax.ShapeDtypeStruct(shape, dtype)


def forward(plan, received, xt, place, live, qgain, ogain):
    width = xt.shape[1]
    blocks = received.shape[1]
    ins = [
        SMEM,
        vmem((1, blocks, 128, 128), (0, 0, 0, 0)),
        vmem((2, blocks, TAIL, 128), (0, 0, 128 // TAIL, 0)),
        whole((HEAD, width)),
        whole(place.shape),
        whole((1, width)),
        whole((HEAD, 1)),
        whole((HEAD, 1)),
    ]
    outs = [
        plain((HEAD, width), BF16),
        plain((blocks, width // 128, 128)),
        plain((DOCS + 1, 8, TILE)),
        plain((HEAD, width)),
        plain((HEAD, width)),
        plain((1, width)),
    ]
    return call(
        forward_kernel, "forward", ins, outs, forward_scratch(items_of(blocks * 128)),
        (plan, received, received, xt, place, live, qgain, ogain),
    )


def backward_step(keyval, probs, grad_probs, delta, pair, grad_kv_ref, c):
    grad_scores = (probs * (grad_probs - delta)).astype(BF16)
    left = jnp.concatenate([grad_scores, probs.astype(BF16)], axis=1)
    per = CHUNK // 128
    held = grad_kv_ref[0, pl.ds(c * per, per)].reshape(CHUNK, 128)
    added = held.astype(F32) + dot(left, pair, 1, 0)
    grad_kv_ref[0, pl.ds(c * per, per)] = added.astype(BF16).reshape(per, 128, 128)
    return dot(keyval, grad_scores, 0, 0)[:HEAD]


def fill_pairs(pair_ref, delta_ref, query, grad_out, deltas):
    keys_side = upright(query.astype(F32) * SCALE)
    values_side = upright(grad_out)
    for d in range(DOCS):
        s = lanes(d)
        pair_ref[d] = jnp.concatenate([keys_side[s], values_side[s]], axis=0)
        delta_ref[d] = jnp.broadcast_to(deltas[:, s], (8, TILE))
    pair_ref[DOCS] = jnp.zeros((2 * TILE, 128), BF16)
    delta_ref[DOCS] = jnp.zeros((8, TILE), F32)


def backward_scratch():
    return [
        pltpu.VMEM((DOCS + 1, 2 * TILE, 128), BF16),
        pltpu.VMEM((DOCS + 1, 8, TILE), F32),
        pltpu.VMEM((DOCS + 1, HEAD, TILE), F32),
    ]


def lined_up(ref):
    return jnp.concatenate([ref[d] for d in range(DOCS)], axis=1)


def middle_kernel(
    plan_ref, kv_ref, sums_ref, xt_ref, live_ref, qgain_ref, ogain_ref, gt_ref,
    grad_kv_ref, out_ref, cross_ref, grad_norm_ref, inv_ref, grad_qg_ref, grad_og_ref,
    total_ref, query_ref, top_ref, norm_ref, store,
    pair_ref, delta_ref, grad_query_ref, lse_ref, grad_ref,
):
    grad_kv_ref[...] = jnp.zeros_like(grad_kv_ref)
    grad_query_ref[...] = jnp.zeros_like(grad_query_ref)
    total = total_of(sums_ref)
    xt = xt_ref[...].astype(F32)
    inv, low = normed_query(xt, total, qgain_ref[...])
    inv_ref[...] = inv
    query = pad_low(low)
    grad = gt_ref[...].astype(F32)
    grad_low = (grad * ogain_ref[...]).astype(BF16)
    grad_out = pad_high(grad_low)
    for d in range(DOCS):
        grad_ref[d] = grad_out[:, lanes(d)]
    grad_ref[DOCS] = jnp.zeros((128, TILE), BF16)
    forward_items(
        plan_ref, kv_ref, query, lse_ref, total_ref, query_ref, top_ref, norm_ref, store
    )
    both = [attended(total_ref, d) for d in range(DOCS)]
    attn = jnp.concatenate([a for a, _ in both], axis=1)
    exact = jnp.concatenate([e for _, e in both], axis=1)
    deltas = jnp.sum(grad_low.astype(F32) * exact, axis=0, keepdims=True)
    fill_pairs(pair_ref, delta_ref, query, grad_out, deltas)

    def back(k):
        c, d = plan_ref[0, k], plan_ref[1, k]
        keyval = chunk_of(kv_ref, c)
        probs = jnp.exp2(store[k] - lse_ref[d, 0:1])
        grad_probs = dot(keyval, grad_ref[d], 1, 0)
        grad_query_ref[d] += backward_step(
            keyval, probs, grad_probs, delta_ref[d, 0:1], pair_ref[d], grad_kv_ref, c
        )

    work(kv_ref.shape[1] * 128, back)
    out_ref[...] = ((xt + ogain_ref[...] * attn) * live_ref[...]).astype(BF16)
    grad_query = lined_up(grad_query_ref) * SCALE
    grad_norm = grad_query * qgain_ref[...]
    grad_norm_ref[...] = grad_norm
    cross = jnp.sum(grad_norm * xt, axis=0, keepdims=True)
    cross_ref[...] = as_messages(cross, cross_ref.shape)
    grad_qg_ref[...] = jnp.sum(grad_query * (xt * inv), axis=1, keepdims=True)
    grad_og_ref[...] = jnp.sum(grad * attn, axis=1, keepdims=True)


def middle(plan, received, sums, xt, live, qgain, ogain, gt):
    width = xt.shape[1]
    blocks = received.shape[1]
    ins = [
        SMEM,
        vmem((1, blocks, 128, 128), (1, 0, 0, 0)),
        whole((blocks, width // 128, 128)),
        whole((HEAD, width)),
        whole((1, width)),
        whole((HEAD, 1)),
        whole((HEAD, 1)),
        whole((HEAD, width)),
    ]
    outs = [
        (
            vmem((1, blocks, 128, 128), (1, 0, 0, 0)),
            jax.ShapeDtypeStruct((2, blocks, 128, 128), BF16),
        ),
        plain((HEAD, width), BF16),
        plain((blocks, width // 128, 128)),
        plain((HEAD, width)),
        plain((1, width)),
        plain((HEAD, 1)),
        plain((HEAD, 1)),
    ]
    scratch = forward_scratch(items_of(blocks * 128)) + backward_scratch()
    scratch += [
        pltpu.VMEM((DOCS + 1, 8, TILE), F32),
        pltpu.VMEM((DOCS + 1, 128, TILE), BF16),
    ]
    return call(
        middle_kernel, "middle", ins, outs, scratch,
        (plan, received, sums, xt, live, qgain, ogain, gt),
    )


def backward_kernel(
    plan_ref, kv_ref, cross_ref, gt_ref, grad_norm_ref, xt1_ref, inv1_ref,
    xt_ref, inv_ref, lse_ref, attn_ref, exact_ref, qgain_ref, ogain_ref, held_ref,
    grad_kv_ref, grad_qg_ref, grad_og_ref, pair_ref, delta_ref, grad_query_ref, both_ref,
):
    del held_ref
    grad_kv_ref[...] = jnp.zeros_like(grad_kv_ref)
    grad_query_ref[...] = jnp.zeros_like(grad_query_ref)
    cross = total_of(cross_ref)
    inv1 = inv1_ref[...]
    xt1 = xt1_ref[...].astype(F32)
    grad = gt_ref[...].astype(F32) + inv1 * grad_norm_ref[...]
    grad = (grad - xt1 * (inv1 * inv1 * inv1) * (cross / D)).astype(BF16).astype(F32)
    grad_low = (grad * ogain_ref[...]).astype(BF16)
    grad_out = pad_high(grad_low)
    grad_og_ref[...] = jnp.sum(grad * attn_ref[...], axis=1, keepdims=True)
    deltas = jnp.sum(grad_low.astype(F32) * exact_ref[...], axis=0, keepdims=True)
    normed = xt_ref[...].astype(F32) * inv_ref[...]
    query = pad_low((normed * qgain_ref[...]).astype(BF16))
    fill_pairs(pair_ref, delta_ref, query, grad_out, deltas)
    for d in range(DOCS):
        both_ref[d] = jnp.concatenate([query[:, lanes(d)], grad_out[:, lanes(d)]], axis=1)
    both_ref[DOCS] = jnp.zeros((128, 2 * TILE), BF16)

    def back(k):
        c, d = plan_ref[0, k], plan_ref[1, k]
        keyval = chunk_of(kv_ref, c)
        product = dot(keyval, both_ref[d], 1, 0)
        scores = logits(product[:, :TILE], c, plan_ref[2, k], plan_ref[3, k])
        probs = jnp.exp2(scores - lse_ref[d, 0:1])
        grad_query_ref[d] += backward_step(
            keyval, probs, product[:, TILE:], delta_ref[d, 0:1], pair_ref[d], grad_kv_ref, c
        )

    work(kv_ref.shape[1] * 128, back)
    grad_query = lined_up(grad_query_ref) * SCALE
    grad_qg_ref[...] = jnp.sum(grad_query * normed, axis=1, keepdims=True)


def backward(
    plan, received, cross, gt, grad_norm, xt1, inv1, xt, inv, lse, attn, exact, qgain, ogain, held
):
    width = xt.shape[1]
    blocks = received.shape[1]
    ins = [
        SMEM,
        vmem((1, blocks, 128, 128), (0, 0, 0, 0)),
        whole((blocks, width // 128, 128)),
        whole((HEAD, width)),
        whole((HEAD, width)),
        whole((HEAD, width)),
        whole((1, width)),
        whole((HEAD, width)),
        whole((1, width)),
        whole(lse.shape),
        whole((HEAD, width)),
        whole((HEAD, width)),
        whole((HEAD, 1)),
        whole((HEAD, 1)),
        pl.BlockSpec(memory_space=pl.ANY),
    ]
    outs = [
        (
            vmem((1, blocks, 128, 128), (0, 0, 0, 0)),
            jax.ShapeDtypeStruct(held.shape, BF16),
        ),
        plain((HEAD, 1)),
        plain((HEAD, 1)),
    ]
    scratch = backward_scratch() + [pltpu.VMEM((DOCS + 1, 128, 2 * TILE), BF16)]
    return call(
        backward_kernel, "backward", ins, outs, scratch,
        (plan, received, cross, gt, grad_norm, xt1, inv1, xt, inv, lse, attn, exact,
         qgain, ogain, held),
        input_output_aliases={14: 0},
    )


def runs(seg):
    counts = [jnp.sum((seg < d).astype(jnp.int32)) for d in range(1, DOCS)]
    return jnp.stack([jnp.int32(0)] + counts + [jnp.int32(seg.shape[0])])


def plan_of(kseg):
    edges = runs(kseg)
    first, last = edges[:-1], edges[1:]
    start = first // CHUNK
    count = (last + (CHUNK - 1)) // CHUNK - start
    ends = jnp.cumsum(count)
    k = jnp.arange(items_of(kseg.shape[0]), dtype=jnp.int32)
    doc = jnp.sum((k[:, None] >= ends[None, :]).astype(jnp.int32), axis=1)
    chunk, low, high = jnp.zeros_like(k), jnp.zeros_like(k), jnp.full_like(k, kseg.shape[0])
    for d in range(DOCS):
        here = doc == d
        chunk = jnp.where(here, start[d] + k - (ends[d] - count[d]), chunk)
        low = jnp.where(here, first[d], low)
        high = jnp.where(here, last[d], high)
    return jnp.stack([chunk, doc, low, high])


def place_of(qseg):
    edges = runs(qseg)
    lane = jnp.arange(TILE, dtype=jnp.int32)
    row = (edges[:-1, None] + lane[None, :]).reshape(1, DOCS * TILE)
    live = (lane[None, :] < (edges[1:] - edges[:-1])[:, None]).reshape(1, DOCS * TILE)
    rows = jnp.arange(qseg.shape[0], dtype=jnp.int32)[:, None]
    return ((rows == row) & live).astype(BF16), live.astype(F32)


def placed(x, place):
    return lax.dot_general(
        x, place, (((0,), (0,)), ((), ())), preferred_element_type=F32
    ).astype(BF16)


def taken(xt, place):
    return lax.dot_general(
        place, xt, (((1,), (1,)), ((), ())), preferred_element_type=F32
    ).astype(BF16)


def swap(value):
    return lax.ppermute(value, "phase", [(0, 1), (1, 0)])


def spread(value):
    return lax.all_to_all(value, "seq", 0, 0, tiled=True)


def local(dec_in, enc_kv, dec_seg, enc_seg, q_gain, o_gain, cotangent):
    phase = lax.axis_index("phase")
    first_phase = phase == 0
    micro = dec_in.shape[0]
    positions = enc_seg.shape[1]
    blocks = positions // 128

    sent = pack(phase.reshape(1), enc_kv[0], jnp.transpose(dec_in, (0, 2, 1)))
    own = jnp.concatenate([q_gain, o_gain], axis=0)
    other = swap(own)
    received = lax.all_to_all(sent, BOTH, 0, 0, tiled=True)
    received = received.reshape(2, blocks, 128 + TAIL, 128)

    gains0 = jnp.where(first_phase, own, other)
    gains1 = jnp.where(first_phase, other, own)
    qgain0, ogain0 = gains0[0][:, None], gains0[1][:, None]
    qgain1, ogain1 = gains1[0][:, None], gains1[1][:, None]
    qseg = lax.dynamic_index_in_dim(dec_seg, phase, 0, keepdims=False)
    kseg = lax.dynamic_index_in_dim(enc_seg, phase, 0, keepdims=False)
    plan = plan_of(kseg)
    place, live = place_of(qseg)
    xt0 = placed(lax.dynamic_index_in_dim(dec_in, phase, 0, keepdims=False), place)
    gt = placed(lax.dynamic_index_in_dim(cotangent, phase, 0, keepdims=False), place)

    xt1, sums, lse0, attn0, exact0, inv0 = forward(
        plan, received, xt0, place, live, qgain0, ogain0
    )
    sums = spread(sums)
    grad_kv, xt2, cross, grad_norm, inv1, grad_qg1, grad_og1 = middle(
        plan, received, sums, xt1, live, qgain1, ogain1, gt
    )
    cross = spread(cross)
    grad_kv, grad_qg0, grad_og0 = backward(
        plan, received, cross, gt, grad_norm, xt1, inv1, xt0, inv0, lse0, attn0, exact0,
        qgain0, ogain0, grad_kv,
    )
    rows_back = lax.all_to_all(
        grad_kv.reshape(2 * blocks, 128, 128), BOTH, 0, 0, tiled=True
    )
    grad_rows = unpack(rows_back, micro)

    out0, out1 = taken(xt1, place), taken(xt2, place)
    mine = jnp.where(first_phase, out0, out1)
    theirs = swap(jnp.where(first_phase, out1, out0))
    sect_out = jnp.where(
        first_phase, jnp.stack([mine, theirs]), jnp.stack([theirs, mine])
    )
    grads0 = jnp.concatenate([grad_qg0, grad_og0], axis=1).T
    grads1 = jnp.concatenate([grad_qg1, grad_og1], axis=1).T
    grads = jnp.where(first_phase, grads0, grads1) + swap(
        jnp.where(first_phase, grads1, grads0)
    )
    return (sect_out[None], grad_rows[None], grads[0:1], grads[1:2])


def solution(mesh):
    in_specs = (
        P(None, None, "seq"),
        P("phase", None, "seq", None),
        P(),
        P(),
        P("phase", "seq"),
        P("phase", "seq"),
        P(None, None, "seq"),
    )
    out_specs = (
        P("phase", None, None, "seq"),
        P("phase", None, "seq", None),
        P("phase", "seq"),
        P("phase", "seq"),
    )
    return jax.shard_map(local, mesh=mesh, in_specs=in_specs, out_specs=out_specs, check_vma=False)
```
